256 devices in a mesh: tm: 32 (over z, x), space: 8 (over y, core).
Axes of the slice: x: 4, y: 4, z: 8, core: 2. Of those that a mesh axis runs over, the one named last changes fastest.
Arguments:
- sources: float32 [64, 4, 1024, 256], P('tm', None, 'space'), may hold values from -36 to 36
- starts: float32 [64, 1024, 256], P('tm', 'space'), may hold values from -24 to 24
- coupling: float32 [1024], P('space'), may hold values from 0.05 to 0.25
- classes: int32 [1024, 2], P('space'), may hold values from 0 to 3
- inverses: float32 [4, 128, 128], replicated, may hold values from 0 to 1
- coarse_rate: float32 [4, 128], replicated, may hold values from 0.002 to 0.5
Outputs:
- states: float32 [64, 4, 1024, 256], P('tm', None, 'space')
The draws below stay inside these ranges and needn't reach their ends.
All inputs are finite; a program needn't handle non-finite values.
Results may differ from the reference program's by a relative error of at most 0.0003.
Values sent between devices are 32-bit elements; how exact they have to be, the bound alone decides.
No kernel may reach another device: no remote copies, remote signals or barrier semaphores. Data moves between devices by JAX's collectives and lax.ppermute only.
A program may use at most 64 MiB of HBM per device.

```python
import math
import jax
import jax.numpy as jnp
from jax import lax

LB = 128
BLOCKS = 2
STEPS = 4
CLASSES = 4
LINE = 256
ROWS = 1024
GROUPS = 64


def draw_inverses(key, part):
    first_key, second_key = jax.random.split(jax.random.fold_in(key, 17))
    cond_lo, cond_hi, leak_lo, leak_hi = (150.0, 1500.0, 0.01, 0.1)
    conduct = jnp.exp(jax.random.uniform(first_key, (CLASSES, LB - 1), jnp.float32, jnp.log(cond_lo), jnp.log(cond_hi)))
    leakage = jnp.exp(jax.random.uniform(second_key, (CLASSES, LB), jnp.float32, jnp.log(leak_lo), jnp.log(leak_hi)))
    left_side = jnp.pad(conduct, ((0, 0), (1, 0)))
    right_side = jnp.pad(conduct, ((0, 0), (0, 1)))
    diagonal = 1.5 + leakage + left_side + right_side
    identity = jnp.eye(LB, dtype=jnp.float32)
    upper = jnp.eye(LB, k=1, dtype=jnp.float32)
    lower = jnp.eye(LB, k=-1, dtype=jnp.float32)
    matrix = diagonal[:, :, None] * identity - right_side[:, :, None] * upper - left_side[:, :, None] * lower
    return jnp.linalg.inv(matrix).astype(jnp.float32)


def place_ends(entries, key, least, high):
    extent = entries.shape
    place = [jax.random.randint(jax.random.fold_in(key, axis), (), 0, extent[axis]) for axis in range(len(extent))]
    entries = entries.at[tuple(place)].set(least)
    longest = extent.index(max(extent))
    place[longest] = (place[longest] + 1) % extent[longest]
    return entries.at[tuple(place)].set(high)


def steps_of(own_key, dims, cuts, low, high):
    factor_of, own = 1.0, jax.random.fold_in(own_key, 6)
    for dim, shards_of in cuts:
        steps = jnp.exp(jax.random.uniform(jax.random.fold_in(own, dim), (shards_of,), jnp.float32, low / len(cuts), high / len(cuts)))
        factor_of = factor_of * jnp.repeat(steps, dims[dim] // shards_of).reshape([-1 if axis == dim else 1 for axis in range(len(dims))])
    return factor_of


def noise(stream_key, shape, scale, limit, cuts=(), held_as=jnp.bfloat16):
    array = scale * jax.random.normal(stream_key, shape, jnp.float32)
    if cuts:
        array = array * steps_of(stream_key, shape, cuts, -0.22, 0.18)
    return jnp.clip(array, -limit, limit).astype(held_as)


def setup_inputs(seed: int = 0) -> dict:
    arg_keys = jax.random.split(jax.random.key(seed), 7)
    return {
        "sources": noise(arg_keys[0], (GROUPS, STEPS, ROWS, LINE), 6.0, 36.0, ((0, 32), (2, 8)), jnp.float32),
        "starts": noise(arg_keys[1], (GROUPS, ROWS, LINE), 4.0, 24.0, ((0, 32), (1, 8)), jnp.float32),
        "coupling": jnp.clip(0.05 + 0.2 * jax.random.uniform(arg_keys[2], (ROWS,), jnp.float32) ** steps_of(arg_keys[2], (ROWS,), ((0, 8),), -0.2, 0.2), 0.05, 0.25),
        "classes": place_ends(jax.random.randint(arg_keys[3], (ROWS, BLOCKS), 0, CLASSES), jax.random.fold_in(arg_keys[3], 1), 0, CLASSES - 1).astype(jnp.int32),
        "inverses": draw_inverses(jax.random.fold_in(arg_keys[6], 71), 0),
        "coarse_rate": jnp.clip(jnp.exp(jax.random.uniform(arg_keys[5], (CLASSES, LB), jnp.float32, math.log(0.002), math.log(0.5))), 0.002, 0.5),
    }


def advance(field, source, coupling, table):
    padded = jnp.pad(field, ((0, 0), (1, 1), (0, 0)))
    rhs = field + coupling[None, :, None] * (padded[:, :-2] + padded[:, 2:]) + source
    group_count, row_count, line_len = rhs.shape
    blocked = rhs.reshape(group_count, row_count, line_len // LB, LB)
    result = jnp.einsum('krbj,rbij->krbi', blocked, table, precision=lax.Precision.HIGHEST)
    return result.reshape(group_count, row_count, line_len)

def reference(sources, starts, coupling, classes, inverses, coarse_rate):
    table = inverses[classes]
    decay = jnp.exp(-coarse_rate[classes]).reshape(ROWS, LINE)
    fine_state = starts
    for substep in range(STEPS - 1):
        fine_state = advance(fine_state, sources[:, substep], coupling, table)
    ends = advance(fine_state, sources[:, STEPS - 1], coupling, table)
    new_starts = jnp.concatenate([starts[:1], ends[:-1]], axis=0)
    fine_state = new_starts
    for substep in range(STEPS - 1):
        fine_state = advance(fine_state, sources[:, substep], coupling, table)
    resid = advance(fine_state, sources[:, STEPS - 1], coupling, table) - ends

    def link(carried, term):
        carried = decay * carried + term
        return (carried, carried)
    _, errors = lax.scan(link, jnp.zeros((ROWS, LINE), jnp.float32), resid)
    finals = ends + errors
    fine_state = jnp.concatenate([starts[:1], finals[:-1]], axis=0)
    collected = []
    for substep in range(STEPS - 1):
        fine_state = advance(fine_state, sources[:, substep], coupling, table)
        collected.append(fine_state)
    collected.append(finals)
    return jnp.stack(collected, axis=1)
```

```python
import functools

import jax
import jax.numpy as jnp
from jax import lax
from jax.experimental import pallas as pl
from jax.experimental.pallas import tpu as pltpu
from jax.sharding import PartitionSpec as P

LB = 128
PAD = 16
EDGE = 8
VMEM = pl.BlockSpec(memory_space=pltpu.VMEM)
SMEM = pl.BlockSpec(memory_space=pltpu.SMEM)


def class_masks(params):
    even, odd, upper = [], [], []
    for block in range(2):
        category = jnp.broadcast_to(params[:, 1 + block : 2 + block], (params.shape[0], LB))
        high = category > 1.5
        low = category - jnp.where(high, 2.0, 0.0)
        odd.append(jnp.where(low > 0.5, 1.0, 0.0).astype(jnp.bfloat16))
        even.append(jnp.where(low > 0.5, 0.0, 1.0).astype(jnp.bfloat16))
        upper.append(high)
    return even, odd, upper


def cut_masks(masks, first, last):
    return tuple([m[first:last] for m in kind] for kind in masks)


def solve_lines(fields, masks, weights):
    even, odd, upper = masks
    rows = fields[0].shape[0]
    left = []
    for field in fields:
        for block in range(2):
            x = field[:, block * LB : (block + 1) * LB]
            high = x.astype(jnp.bfloat16)
            low = (x - high.astype(jnp.float32)).astype(jnp.bfloat16)
            high_pair = [high * even[block], high * odd[block]]
            low_pair = [low * even[block], low * odd[block]]
            left.append(jnp.concatenate(high_pair + low_pair + high_pair, axis=1))
    product = jnp.dot(jnp.concatenate(left, axis=0), weights, preferred_element_type=jnp.float32)
    results = []
    for index in range(len(fields)):
        blocks = []
        for block in range(2):
            part = product[(2 * index + block) * rows : (2 * index + block + 1) * rows]
            blocks.append(jnp.where(upper[block], part[:, LB:], part[:, :LB]))
        results.append(jnp.concatenate(blocks, axis=1))
    return results


def spread(field, coupling):
    rows = field.shape[0]
    return field + coupling * (pltpu.roll(field, 1, 0) + pltpu.roll(field, rows - 1, 0))


def relax_kernel(
    chunks, first_ref, starts_ref, sources_ref, params_ref, above_ref, below_ref, weights_ref, rates_ref,
    terms_ref, factor_ref, shift_ref, decay_ref, base_ref, last_ref, relaxed_ref,
):
    first = first_ref[0, 0]

    def padded(slab, own):
        return jnp.concatenate([above_ref[slab], own, below_ref[slab]], axis=0)

    params = padded(10, params_ref[...])
    coupling = jnp.broadcast_to(params[:, :1], (params.shape[0], 2 * LB))
    masks = class_masks(params)
    rows = params.shape[0]
    near = slice(EDGE, rows - EDGE)
    own = slice(PAD, rows - PAD)
    near_coupling, near_masks = coupling[near], cut_masks(masks, EDGE, rows - EDGE)
    weights = weights_ref[...]

    starts = [padded(g * 5, starts_ref[g]) for g in range(2)]

    def source(g, m):
        return padded(g * 5 + 1 + m, sources_ref[g, m])

    linear = starts[0][near]
    state = starts
    for m in range(2):
        state = solve_lines([spread(state[g], coupling) + source(g, m) for g in range(2)], masks, weights)
        (linear,) = solve_lines([spread(linear, near_coupling)], near_masks, weights)
        for g in range(2):
            relaxed_ref[g, m] = state[g][own]
    rhs = [(spread(state[g], coupling) + source(g, 2))[near] for g in range(2)]
    *state, linear = solve_lines(rhs + [spread(linear, near_coupling)], near_masks, weights)
    inner = slice(EDGE, rows - EDGE - PAD)
    for g in range(2):
        relaxed_ref[g, 2] = state[g][inner]
    rhs = [spread(state[g], near_coupling) + source(g, 3)[near] for g in range(2)]
    *ends, linear = solve_lines(rhs + [spread(linear, near_coupling)], near_masks, weights)
    linear = jnp.where(first > 0, jnp.zeros_like(linear), linear)

    change = ends[0] - starts[1][near]
    resid, onward = change, ends[1]
    for m in range(4):
        resid, onward = solve_lines(
            [spread(resid, near_coupling), spread(onward, near_coupling)], near_masks, weights
        )

    near_params = params[near]
    rate_blocks = []
    for block in range(2):
        category = jnp.broadcast_to(near_params[:, 1 + block : 2 + block], (near_params.shape[0], LB))
        rate = jnp.broadcast_to(rates_ref[0:1, :], category.shape)
        for c in range(1, 4):
            rate = jnp.where(category > c - 0.5, jnp.broadcast_to(rates_ref[c : c + 1, :], category.shape), rate)
        rate_blocks.append(rate)
    rates = jnp.concatenate(rate_blocks, axis=1)
    decay = jnp.exp(-rates)
    ahead = onward * jnp.exp(rates)
    term = resid + ahead - decay * linear

    tiles = term.shape[0] // 8
    terms_ref[...] = jnp.zeros_like(terms_ref)
    factor_ref[...] = jnp.zeros_like(factor_ref)
    squared = decay * decay
    for block in range(2):
        for t in range(tiles):
            tile = block * tiles + t
            chunk, slot = tile % chunks, tile // chunks
            where = (slice(t * 8, t * 8 + 8), slice(block * LB, (block + 1) * LB))
            terms_ref[chunk, slot * 8 : slot * 8 + 8, :] = term[where]
            factor_ref[chunk, slot * 8 : slot * 8 + 8, :] = squared[where]
    shift_ref[...] = ends[1] - ahead
    decay_ref[...] = decay
    base_ref[0] = jnp.where(first > 0, jnp.zeros_like(linear), starts[0][near])
    base_ref[1] = change - linear
    last_ref[0] = ends[0][inner] - linear[inner]
    last_ref[1] = (ends[1] + resid - decay * linear)[inner]


def scan_kernel(terms_ref, factor_ref, entering_ref):
    factor = factor_ref[...]
    carried = jnp.zeros_like(factor)
    for d in range(terms_ref.shape[0]):
        entering_ref[d] = carried
        carried = factor * carried + terms_ref[d]


def final_kernel(
    chunks, entering_ref, shift_ref, decay_ref, base_ref, last_ref, relaxed_ref, params_ref, above_ref, below_ref,
    weights_ref, states_ref,
):
    decay = decay_ref[...]
    tiles = decay.shape[0] // 8
    blocks = []
    for block in range(2):
        parts = []
        for t in range(tiles):
            tile = block * tiles + t
            chunk, slot = tile % chunks, tile // chunks
            parts.append(entering_ref[chunk, slot * 8 : slot * 8 + 8, :])
        blocks.append(jnp.concatenate(parts, axis=0))
    entering = jnp.concatenate(blocks, axis=1)
    params = jnp.concatenate([above_ref[10][EDGE:], params_ref[...], below_ref[10][:EDGE]], axis=0)
    coupling = jnp.broadcast_to(params[:, :1], (params.shape[0], 2 * LB))
    masks = class_masks(params)
    inner = slice(EDGE, params.shape[0] - EDGE)
    passed = decay * entering
    states_ref[0, 3] = passed[inner] + last_ref[0]
    states_ref[1, 3] = (decay * passed)[inner] + last_ref[1]
    state = [entering + shift_ref[...] - base_ref[0], passed + base_ref[1]]
    weights = weights_ref[...]
    for m in range(3):
        state = solve_lines([spread(s, coupling) for s in state], masks, weights)
        for g in range(2):
            states_ref[g, m] = relaxed_ref[g, m] + state[g][inner]


def shards(sources, starts, coupling, classes, inverses, coarse_rate):
    count, along = lax.axis_size("tm"), lax.axis_size("space")
    lines, line_len = starts.shape[1:]
    near_rows = lines + 2 * EDGE
    f32 = jnp.float32
    first = (lax.axis_index("tm") == 0).astype(jnp.int32).reshape(1, 1)

    params = jnp.concatenate([coupling[:, None], classes.astype(f32)], axis=1)
    params = jnp.pad(params, ((0, 0), (0, line_len - 3)))

    def slabs(rows):
        fields = jnp.concatenate([starts[:, None, rows], sources[:, :, rows]], axis=1)
        fields = fields.reshape(-1, PAD, line_len)
        return jnp.concatenate([fields, params[None, rows]], axis=0)

    with jax.named_scope("halo"):
        up = [(i, i + 1) for i in range(along - 1)]
        down = [(j, i) for i, j in up]
        above = lax.ppermute(slabs(slice(lines - PAD, lines)), "space", up)
        below = lax.ppermute(slabs(slice(0, PAD)), "space", down)

    with jax.named_scope("weights"):
        transposed = inverses.transpose(0, 2, 1)
        table = jnp.concatenate(
            [
                jnp.concatenate([transposed[0], transposed[2]], axis=1),
                jnp.concatenate([transposed[1], transposed[3]], axis=1),
            ],
            axis=0,
        )
        high = lax.reduce_precision(table, 8, 7)
        weights = jnp.concatenate([high, high, table - high], axis=0).astype(jnp.bfloat16)

    per_chunk = 8 * -(-(2 * near_rows // 8) // count)
    chunked = jax.ShapeDtypeStruct((count, per_chunk, LB), f32)
    near = jax.ShapeDtypeStruct((near_rows, line_len), f32)
    params_compiler = pltpu.CompilerParams(vmem_limit_bytes=48 * 1024 * 1024)
    terms, factors, shift, decay, base, last, relaxed = pl.pallas_call(
        functools.partial(relax_kernel, count),
        out_shape=(
            chunked,
            chunked,
            near,
            near,
            jax.ShapeDtypeStruct((2, near_rows, line_len), f32),
            jax.ShapeDtypeStruct((2, lines, line_len), f32),
            jax.ShapeDtypeStruct((2, 3, lines, line_len), f32),
        ),
        in_specs=[SMEM] + [VMEM] * 7,
        out_specs=[VMEM] * 7,
        compiler_params=params_compiler,
        name="relax",
    )(first, starts, sources, params, above, below, weights, coarse_rate)

    with jax.named_scope("onward"):
        shift = lax.ppermute(shift, "tm", [(i, i + 1) for i in range(count - 1)])
    with jax.named_scope("gather_terms"):
        terms = lax.all_to_all(terms, "tm", 0, 0)
    factor = lax.dynamic_index_in_dim(factors, lax.axis_index("tm"), 0, keepdims=False)
    entering = pl.pallas_call(
        scan_kernel,
        out_shape=chunked,
        in_specs=[VMEM] * 2,
        out_specs=VMEM,
        compiler_params=params_compiler,
        name="scan",
    )(terms, factor)
    with jax.named_scope("return_terms"):
        entering = lax.all_to_all(entering, "tm", 0, 0)
    return pl.pallas_call(
        functools.partial(final_kernel, count),
        out_shape=jax.ShapeDtypeStruct((2, 4, lines, line_len), f32),
        in_specs=[VMEM] * 10,
        out_specs=VMEM,
        compiler_params=params_compiler,
        name="final",
    )(entering, shift, decay, base, last, relaxed, params, above, below, weights)


def solution(mesh):
    in_specs = (
        P("tm", None, "space", None),
        P("tm", "space", None),
        P("space"),
        P("space", None),
        P(),
        P(),
    )
    out_specs = P("tm", None, "space", None)
    return jax.shard_map(shards, mesh=mesh, in_specs=in_specs, out_specs=out_specs, check_vma=False)
```

```python
import functools

import jax
import jax.numpy as jnp
from jax import lax
from jax.experimental import pallas as pl
from jax.experimental.pallas import tpu as pltpu
from jax.sharding import PartitionSpec as P

LB = 128
GROUPS = 2
STEPS = 4
SLAB = 16
EDGE = 8
SIDE = 4
REACH = (11, 10, 9, 8, 7)
GROUP_ROWS = sum(REACH)
MESSAGE_ROWS = 96
VMEM = pl.BlockSpec(memory_space=pltpu.VMEM)
SMEM = pl.BlockSpec(memory_space=pltpu.SMEM)
HBM = pl.BlockSpec(memory_space=pltpu.HBM)
VMEM_LIMIT = 32 * 1024 * 1024


def columns(row):
    return jnp.broadcast_to(row, (LB, LB)).T


def class_masks(categories):
    even, odd, upper = [], [], []
    for category in categories:
        high = category > 1.5
        low = category - jnp.where(high, 2.0, 0.0)
        odd.append(jnp.where(low > 0.5, 1.0, 0.0).astype(jnp.bfloat16))
        even.append(jnp.where(low > 0.5, 0.0, 1.0).astype(jnp.bfloat16))
        upper.append(high)
    return even, odd, upper


def rates_of(categories, rates_ref):
    blocks = []
    for category in categories:
        rate = jnp.broadcast_to(rates_ref[0:1, :], category.shape)
        for c in range(1, 4):
            rate = jnp.where(category > c - 0.5, jnp.broadcast_to(rates_ref[c : c + 1, :], category.shape), rate)
        blocks.append(rate)
    return jnp.concatenate(blocks, axis=1)


def solve_lines(fields, masks, weights):
    even, odd, upper = masks
    rows = fields[0].shape[0]
    left = []
    for field in fields:
        for block in range(2):
            x = field[:, block * LB : (block + 1) * LB]
            high = x.astype(jnp.bfloat16)
            low = (x - high.astype(jnp.float32)).astype(jnp.bfloat16)
            high_pair = [high * even[block], high * odd[block]]
            low_pair = [low * even[block], low * odd[block]]
            left.append(jnp.concatenate(high_pair + low_pair + high_pair, axis=1))
    product = jnp.dot(jnp.concatenate(left, axis=0), weights, preferred_element_type=jnp.float32)
    results = []
    for index in range(len(fields)):
        blocks = []
        for block in range(2):
            part = product[(2 * index + block) * rows : (2 * index + block + 1) * rows]
            blocks.append(jnp.where(upper[block], part[:, LB:], part[:, :LB]))
        results.append(jnp.concatenate(blocks, axis=1))
    return results


def spread(field, coupling):
    rows = field.shape[0]
    return field + coupling * (pltpu.roll(field, 1, 0) + pltpu.roll(field, rows - 1, 0))


def relaxations(starts, sources, coupling, categories, weights, rates_ref, first, relaxed_to):
    masks = class_masks(categories)
    linear, state = starts[0], starts
    for m in range(STEPS):
        *state, linear = solve_lines(
            [spread(state[g], coupling) + sources(g, m) for g in range(GROUPS)] + [spread(linear, coupling)],
            masks,
            weights,
        )
        if m < STEPS - 1:
            for g in range(GROUPS):
                relaxed_to(g, m, state[g])
    ends = state
    linear = jnp.where(first > 0, jnp.zeros_like(linear), linear)
    change = ends[0] - starts[1]
    resid, onward = change, ends[1]
    for m in range(STEPS):
        resid, onward = solve_lines([spread(resid, coupling), spread(onward, coupling)], masks, weights)
    rates = rates_of(categories, rates_ref)
    decay = jnp.exp(-rates)
    ahead = onward * jnp.exp(rates)
    held = decay * linear
    return dict(
        term=resid + ahead - held,
        shift=ends[1] - ahead,
        decay=decay,
        bases=(jnp.where(first > 0, jnp.zeros_like(linear), starts[0]), change - linear),
        lasts=(ends[0] - linear, ends[1] + resid - held),
    )


def pack_kernel(
    starts_hbm, sources_hbm, coupling_hbm, classes_hbm, up_ref, down_ref, params_ref,
    starts_low, starts_high, sources_low, sources_high, coupling_row, classes_rows, sems,
):
    lines = starts_hbm.shape[1]
    low, high = pl.ds(0, SLAB), pl.ds(lines - SLAB, SLAB)
    pairs = [
        (sources_hbm.at[:, :, high, :], sources_high),
        (sources_hbm.at[:, :, low, :], sources_low),
        (starts_hbm.at[:, high, :], starts_high),
        (starts_hbm.at[:, low, :], starts_low),
        (coupling_hbm, coupling_row),
        (classes_hbm, classes_rows),
    ]
    copies = [pltpu.make_async_copy(src, dst, sems.at[i]) for i, (src, dst) in enumerate(pairs)]
    for copy in copies:
        copy.start()
    for ref in (up_ref, down_ref, params_ref):
        ref[...] = jnp.zeros_like(ref)
    for copy in copies:
        copy.wait()
    params_ref[0:1, :] = coupling_row[...]
    params_ref[1:3, :] = classes_rows[...].astype(jnp.float32)
    for g in range(GROUPS):
        at = g * GROUP_ROWS
        for index, reach in enumerate(REACH):
            if index == 0:
                up, down = starts_high[g, SLAB - reach :, :], starts_low[g, :reach, :]
            else:
                up, down = sources_high[g, index - 1, SLAB - reach :, :], sources_low[g, index - 1, :reach, :]
            up_ref[at : at + reach, :] = up
            down_ref[at : at + reach, :] = down
            at += reach
    for ref in (up_ref, down_ref):
        ref[GROUPS * GROUP_ROWS : GROUPS * GROUP_ROWS + 3, :LB] = params_ref[0:3, :]


def own_kernel(
    first_ref, starts_ref, sources_ref, params_ref, weights_ref, rates_ref,
    term_ref, shift_ref, decay_ref, base_ref, last_ref, relaxed_ref,
):
    coupling = columns(params_ref[0:1, :])
    coupling = jnp.concatenate([coupling, coupling], axis=1)
    categories = [columns(params_ref[1 + block : 2 + block, :]) for block in range(2)]

    def relaxed_to(g, m, field):
        relaxed_ref[g, m] = field

    out = relaxations(
        [starts_ref[g] for g in range(GROUPS)], lambda g, m: sources_ref[g, m], coupling, categories, weights_ref[...],
        rates_ref, first_ref[0, 0], relaxed_to,
    )
    term_ref[...] = out["term"]
    shift_ref[...] = out["shift"]
    decay_ref[...] = out["decay"]
    for g in range(GROUPS):
        base_ref[g] = out["bases"][g]
        last_ref[g] = out["lasts"][g]


def joined(inner, strip, beyond):
    lines = inner.shape[0]
    return jnp.concatenate([strip[16 - beyond : 24], inner[EDGE : lines - EDGE], strip[40 : 48 + beyond]], axis=0)


def edge_kernel(
    first_ref, starts_ref, sources_ref, params_ref, above_ref, below_ref, weights_ref, rates_ref,
    own_term_ref, own_shift_ref, own_decay_ref,
    terms_ref, factors_ref, decay_ref, base_ref, last_ref, relaxed_ref, halo_ref,
):
    lines = starts_ref.shape[1]
    lane = lax.broadcasted_iota(jnp.int32, (8, LB), 1)
    at = GROUPS * GROUP_ROWS
    own = params_ref[...]
    halo_ref[...] = jnp.zeros_like(halo_ref)
    halo_ref[0, 0:3, :LB] = above_ref[at : at + 3, :LB]
    halo_ref[0, 8:11, :LB] = below_ref[at : at + 3, :LB]
    above, below = halo_ref[0, 0:8, :LB], halo_ref[0, 8:16, :LB]
    upper = jnp.where(lane < SLAB, pltpu.roll(above, SLAB, 1), pltpu.roll(own, SLAB, 1))
    lower = jnp.where(lane < 3 * SLAB, pltpu.roll(own, 3 * SLAB, 1), pltpu.roll(below, 3 * SLAB, 1))
    strip = jnp.where(lane < 2 * SLAB, upper, lower)
    rows = 4 * SLAB
    coupling = columns(strip[0:1])[:rows]
    coupling = jnp.concatenate([coupling, coupling], axis=1)
    categories = [columns(strip[1 + block : 2 + block])[:rows] for block in range(2)]

    halo_ref[0, 0:16, :] = jnp.zeros((16, 2 * LB), jnp.float32)
    for g in range(GROUPS):
        at = g * GROUP_ROWS
        for index, reach in enumerate(REACH):
            slab = g * len(REACH) + index
            halo_ref[slab, SLAB - reach : SLAB, :] = above_ref[at : at + reach, :]
            halo_ref[slab, SLAB : SLAB + reach, :] = below_ref[at : at + reach, :]
            at += reach

    def strips(slab, low, high):
        return jnp.concatenate([halo_ref[slab, :SLAB, :], low, high, halo_ref[slab, SLAB:, :]], axis=0)

    starts = [
        strips(g * len(REACH), starts_ref[g, :SLAB, :], starts_ref[g, lines - SLAB :, :]) for g in range(GROUPS)
    ]

    def sources(g, m):
        return strips(
            g * len(REACH) + 1 + m, sources_ref[g, m, :SLAB, :], sources_ref[g, m, lines - SLAB :, :]
        )

    def relaxed_to(g, m, field):
        relaxed_ref[g, m] = field

    out = relaxations(starts, sources, coupling, categories, weights_ref[...], rates_ref, first_ref[0, 0], relaxed_to)
    section = lines + 2 * SIDE
    decay = joined(own_decay_ref[...], out["decay"], SIDE)
    for index, field in enumerate(
        (joined(own_term_ref[...], out["term"], SIDE), joined(own_shift_ref[...], out["shift"], SIDE))
    ):
        factor = decay * decay if index == 0 else jnp.zeros_like(decay)
        for block in range(2):
            at = (2 * index + block) * section
            lanes = slice(block * LB, (block + 1) * LB)
            terms_ref[at : at + section, :] = field[:, lanes]
            factors_ref[at : at + section, :] = factor[:, lanes]
    decay_ref[...] = out["decay"]
    for g in range(GROUPS):
        base_ref[g] = out["bases"][g]
        last_ref[g] = out["lasts"][g]


def scan_kernel(place_ref, terms_ref, factors_ref, entering_ref):
    factor = factors_ref[place_ref[0, 0]]
    carried = jnp.zeros_like(factor)
    for d in range(terms_ref.shape[0]):
        entering_ref[d] = carried
        carried = factor * carried + terms_ref[d]


def final_kernel(
    entering_ref, params_ref, above_ref, below_ref, weights_ref, decay_ref, base_ref, last_ref, relaxed_ref,
    edge_decay_ref, edge_base_ref, edge_last_ref, edge_relaxed_ref, states_hbm, field_ref, states_ref, sems,
):
    lines = last_ref.shape[1]
    section = lines + 2 * SIDE
    at = GROUPS * GROUP_ROWS

    def along(row):
        own = columns(params_ref[row : row + 1, :])
        above = columns(above_ref[at + row : at + row + 1, :LB])
        below = columns(below_ref[at + row : at + row + 1, :LB])
        return jnp.concatenate([above[lines - EDGE :], own, below[:EDGE]], axis=0)

    coupling = along(0)
    coupling = jnp.concatenate([coupling, coupling], axis=1)
    masks = class_masks([along(1), along(2)])

    gap = EDGE - SIDE
    field_ref[...] = jnp.zeros_like(field_ref)
    for part in range(2):
        for block in range(2):
            start = (2 * part + block) * section
            field_ref[part, gap : gap + section, block * LB : (block + 1) * LB] = entering_ref[start : start + section, :]
    entering, shift = field_ref[0], field_ref[1]
    inner = slice(EDGE, EDGE + lines)
    decay = joined(decay_ref[...], edge_decay_ref[...], EDGE)
    base = [joined(base_ref[g], edge_base_ref[g], EDGE) for g in range(GROUPS)]
    last = [joined(last_ref[g], edge_last_ref[g], 0) for g in range(GROUPS)]
    passed = decay * entering

    def send(m):
        copy = pltpu.make_async_copy(states_ref.at[:, m], states_hbm.at[:, m], sems.at[m])
        copy.start()
        return copy

    states_ref[0, 3] = passed[inner] + last[0]
    states_ref[1, 3] = (decay * passed)[inner] + last[1]
    copies = [send(3)]
    state = [entering + shift - base[0], passed + base[1]]
    weights = weights_ref[...]
    for m in range(STEPS - 1):
        state = solve_lines([spread(s, coupling) for s in state], masks, weights)
        for g in range(GROUPS):
            states_ref[g, m] = joined(relaxed_ref[g, m], edge_relaxed_ref[g, m], 0) + state[g][inner]
        copies.append(send(m))
    for copy in copies:
        copy.wait()


def shards(sources, starts, coupling, classes, inverses, coarse_rate):
    count, along = lax.axis_size("tm"), lax.axis_size("space")
    lines, line_len = starts.shape[1:]
    near_rows, sections = lines + 2 * EDGE, 4 * (lines + 2 * SIDE)
    f32 = jnp.float32
    place = lax.axis_index("tm").astype(jnp.int32).reshape(1, 1)
    first = (lax.axis_index("tm") == 0).astype(jnp.int32).reshape(1, 1)
    grant = pltpu.CompilerParams(vmem_limit_bytes=VMEM_LIMIT)

    def shape(*dims):
        return jax.ShapeDtypeStruct(dims, f32)

    message = shape(MESSAGE_ROWS, line_len)
    up, down, params = pl.pallas_call(
        pack_kernel,
        out_shape=(message, message, shape(8, lines)),
        in_specs=[HBM] * 4,
        out_specs=[VMEM] * 3,
        scratch_shapes=[
            pltpu.VMEM((GROUPS, SLAB, line_len), f32),
            pltpu.VMEM((GROUPS, SLAB, line_len), f32),
            pltpu.VMEM((GROUPS, STEPS, SLAB, line_len), f32),
            pltpu.VMEM((GROUPS, STEPS, SLAB, line_len), f32),
            pltpu.VMEM((1, lines), f32),
            pltpu.VMEM((2, lines), jnp.int32),
            pltpu.SemaphoreType.DMA((6,)),
        ],
        compiler_params=grant,
        name="pack",
    )(*[
        pltpu.with_memory_space_constraint(x, pltpu.HBM)
        for x in (starts, sources, coupling.reshape(1, lines), classes.T)
    ])

    with jax.named_scope("halo"):
        upward = [(i, i + 1) for i in range(along - 1)]
        above = lax.ppermute(up, "space", upward)
        below = lax.ppermute(down, "space", [(j, i) for i, j in upward])

    with jax.named_scope("weights"):
        transposed = inverses.transpose(0, 2, 1)
        table = jnp.concatenate(
            [
                jnp.concatenate([transposed[0], transposed[2]], axis=1),
                jnp.concatenate([transposed[1], transposed[3]], axis=1),
            ],
            axis=0,
        )
        high = lax.reduce_precision(table, 8, 7)
        weights = jnp.concatenate([high, high, table - high], axis=0).astype(jnp.bfloat16)

    def kept(rows):
        return (
            shape(rows, line_len),
            shape(GROUPS, rows, line_len),
            shape(GROUPS, rows, line_len),
            shape(GROUPS, STEPS - 1, rows, line_len),
        )

    term, shift, *own = pl.pallas_call(
        own_kernel,
        out_shape=(shape(lines, line_len), shape(lines, line_len), *kept(lines)),
        in_specs=[SMEM] + [VMEM] * 5,
        out_specs=[VMEM] * 6,
        compiler_params=grant,
        cost_estimate=pl.CostEstimate(flops=5_000_000_000, bytes_accessed=4_000_000, transcendentals=0),
        name="own",
    )(first, starts, sources, params, weights, coarse_rate)
    terms, factors, *edges = pl.pallas_call(
        edge_kernel,
        out_shape=(shape(sections, LB), shape(sections, LB), *kept(4 * SLAB)),
        in_specs=[SMEM] + [VMEM] * 10,
        out_specs=[VMEM] * 6,
        scratch_shapes=[pltpu.VMEM((GROUPS * len(REACH), 2 * SLAB, line_len), f32)],
        compiler_params=grant,
        name="edge",
    )(first, starts, sources, params, above, below, weights, coarse_rate, term, shift, own[0])

    split = (count, 1, sections * LB // count)
    with jax.named_scope("gather_terms"):
        terms = lax.all_to_all(terms.reshape(split), "tm", 0, 0)
    entering = pl.pallas_call(
        scan_kernel,
        out_shape=shape(*split),
        in_specs=[SMEM] + [VMEM] * 2,
        out_specs=VMEM,
        compiler_params=grant,
        name="scan",
    )(place, terms, factors.reshape(split))
    with jax.named_scope("return_terms"):
        entering = lax.all_to_all(entering, "tm", 0, 0)
    return pl.pallas_call(
        final_kernel,
        out_shape=shape(GROUPS, STEPS, lines, line_len),
        in_specs=[VMEM] * 13,
        out_specs=HBM,
        scratch_shapes=[
            pltpu.VMEM((2, near_rows, line_len), f32),
            pltpu.VMEM((GROUPS, STEPS, lines, line_len), f32),
            pltpu.SemaphoreType.DMA((STEPS,)),
        ],
        compiler_params=grant,
        name="final",
    )(entering.reshape(sections, LB), params, above, below, weights, *own, *edges)


def solution(mesh):
    in_specs = (
        P("tm", None, "space", None),
        P("tm", "space", None),
        P("space"),
        P("space", None),
        P(),
        P(),
    )
    out_specs = P("tm", None, "space", None)
    return jax.shard_map(shards, mesh=mesh, in_specs=in_specs, out_specs=out_specs, check_vma=False)
```

```python
import functools

import jax
import jax.numpy as jnp
from jax import lax
from jax.experimental import pallas as pl
from jax.experimental.pallas import tpu as pltpu
from jax.sharding import PartitionSpec as P

LB = 128
GROUPS = 2
STEPS = 4
SLAB = 16
EDGE = 8
REACH = (11, 10, 9, 8, 7)
GROUP_ROWS = sum(REACH)
MESSAGE_ROWS = 96
VMEM = pl.BlockSpec(memory_space=pltpu.VMEM)
SMEM = pl.BlockSpec(memory_space=pltpu.SMEM)
HBM = pl.BlockSpec(memory_space=pltpu.HBM)
MEBI = 1024 * 1024


def columns(row):
    return jnp.broadcast_to(row, (LB, LB)).T


def class_masks(categories):
    even, odd, upper = [], [], []
    for category in categories:
        high = category > 1.5
        low = category - jnp.where(high, 2.0, 0.0)
        odd.append(jnp.where(low > 0.5, 1.0, 0.0).astype(jnp.bfloat16))
        even.append(jnp.where(low > 0.5, 0.0, 1.0).astype(jnp.bfloat16))
        upper.append(high)
    return even, odd, upper


def rates_of(categories, rates_ref):
    blocks = []
    for category in categories:
        rate = jnp.broadcast_to(rates_ref[0:1, :], category.shape)
        for c in range(1, 4):
            rate = jnp.where(category > c - 0.5, jnp.broadcast_to(rates_ref[c : c + 1, :], category.shape), rate)
        blocks.append(rate)
    return jnp.concatenate(blocks, axis=1)


def solve_lines(fields, masks, weights):
    even, odd, upper = masks
    rows = fields[0].shape[0]
    left = []
    for field in fields:
        for block in range(2):
            x = field[:, block * LB : (block + 1) * LB]
            high = x.astype(jnp.bfloat16)
            low = (x - high.astype(jnp.float32)).astype(jnp.bfloat16)
            high_pair = [high * even[block], high * odd[block]]
            low_pair = [low * even[block], low * odd[block]]
            left.append(jnp.concatenate(high_pair + low_pair + high_pair, axis=1))
    product = jnp.dot(jnp.concatenate(left, axis=0), weights, preferred_element_type=jnp.float32)
    results = []
    for index in range(len(fields)):
        blocks = []
        for block in range(2):
            part = product[(2 * index + block) * rows : (2 * index + block + 1) * rows]
            blocks.append(jnp.where(upper[block], part[:, LB:], part[:, :LB]))
        results.append(jnp.concatenate(blocks, axis=1))
    return results


def spread(field, coupling):
    rows = field.shape[0]
    return field + coupling * (pltpu.roll(field, 1, 0) + pltpu.roll(field, rows - 1, 0))


def relaxations(starts, sources, coupling, categories, weights, rates_ref, first, relaxed_to):
    masks = class_masks(categories)
    linear, state = starts[0], starts
    for m in range(STEPS):
        *state, linear = solve_lines(
            [spread(state[g], coupling) + sources(g, m) for g in range(GROUPS)] + [spread(linear, coupling)],
            masks,
            weights,
        )
        if m < STEPS - 1:
            for g in range(GROUPS):
                relaxed_to(g, m, state[g])
    ends = state
    linear = jnp.where(first > 0, jnp.zeros_like(linear), linear)
    change = ends[0] - starts[1]
    resid, onward = change, ends[1]
    for m in range(STEPS):
        resid, onward = solve_lines([spread(resid, coupling), spread(onward, coupling)], masks, weights)
    rates = rates_of(categories, rates_ref)
    decay = jnp.exp(-rates)
    ahead = onward * jnp.exp(rates)
    held = decay * linear
    return dict(
        term=resid + ahead - held,
        shift=ends[1] - ahead,
        decay=decay,
        bases=(jnp.where(first > 0, jnp.zeros_like(linear), starts[0]), change - linear),
        lasts=(ends[0] - linear, ends[1] + resid - held),
    )


def pack_kernel(
    starts_hbm, sources_hbm, coupling_hbm, classes_hbm, up_ref, down_ref, params_ref,
    starts_low, starts_high, sources_low, sources_high, coupling_row, classes_rows, sems,
):
    lines = starts_hbm.shape[1]
    low, high = pl.ds(0, SLAB), pl.ds(lines - SLAB, SLAB)
    pairs = [
        (sources_hbm.at[:, :, high, :], sources_high),
        (sources_hbm.at[:, :, low, :], sources_low),
        (starts_hbm.at[:, high, :], starts_high),
        (starts_hbm.at[:, low, :], starts_low),
        (coupling_hbm, coupling_row),
        (classes_hbm, classes_rows),
    ]
    copies = [pltpu.make_async_copy(src, dst, sems.at[i]) for i, (src, dst) in enumerate(pairs)]
    for copy in copies:
        copy.start()
    for ref in (up_ref, down_ref, params_ref):
        ref[...] = jnp.zeros_like(ref)
    for copy in copies:
        copy.wait()
    params_ref[0:1, :] = coupling_row[...]
    params_ref[1:3, :] = classes_rows[...].astype(jnp.float32)
    for g in range(GROUPS):
        at = g * GROUP_ROWS
        for index, reach in enumerate(REACH):
            if index == 0:
                up, down = starts_high[g, SLAB - reach :, :], starts_low[g, :reach, :]
            else:
                up, down = sources_high[g, index - 1, SLAB - reach :, :], sources_low[g, index - 1, :reach, :]
            up_ref[at : at + reach, :] = up
            down_ref[at : at + reach, :] = down
            at += reach
    for ref in (up_ref, down_ref):
        ref[GROUPS * GROUP_ROWS : GROUPS * GROUP_ROWS + 3, :LB] = params_ref[0:3, :]


def own_kernel(
    first_ref, starts_ref, sources_ref, params_ref, weights_ref, rates_ref,
    term_ref, shift_ref, decay_ref, base_ref, last_ref, relaxed_ref,
):
    coupling = columns(params_ref[0:1, :])
    coupling = jnp.concatenate([coupling, coupling], axis=1)
    categories = [columns(params_ref[1 + block : 2 + block, :]) for block in range(2)]

    def relaxed_to(g, m, field):
        relaxed_ref[g, m] = field

    out = relaxations(
        [starts_ref[g] for g in range(GROUPS)], lambda g, m: sources_ref[g, m], coupling, categories, weights_ref[...],
        rates_ref, first_ref[0, 0], relaxed_to,
    )
    term_ref[...] = out["term"]
    shift_ref[...] = out["shift"]
    decay_ref[...] = out["decay"]
    for g in range(GROUPS):
        base_ref[g] = out["bases"][g]
        last_ref[g] = out["lasts"][g]


def joined(inner, strip, beyond):
    lines = inner.shape[0]
    return jnp.concatenate([strip[16 - beyond : 24], inner[EDGE : lines - EDGE], strip[40 : 48 + beyond]], axis=0)


def edge_kernel(
    first_ref, starts_ref, sources_ref, params_ref, above_ref, below_ref, weights_ref, rates_ref,
    own_term_ref, own_shift_ref, own_decay_ref,
    terms_ref, factors_ref, shift_ref, decay_ref, base_ref, last_ref, relaxed_ref, halo_ref,
):
    lines = starts_ref.shape[1]
    lane = lax.broadcasted_iota(jnp.int32, (8, LB), 1)
    at = GROUPS * GROUP_ROWS
    own = params_ref[...]
    halo_ref[...] = jnp.zeros_like(halo_ref)
    halo_ref[0, 0:3, :LB] = above_ref[at : at + 3, :LB]
    halo_ref[0, 8:11, :LB] = below_ref[at : at + 3, :LB]
    above, below = halo_ref[0, 0:8, :LB], halo_ref[0, 8:16, :LB]
    upper = jnp.where(lane < SLAB, pltpu.roll(above, SLAB, 1), pltpu.roll(own, SLAB, 1))
    lower = jnp.where(lane < 3 * SLAB, pltpu.roll(own, 3 * SLAB, 1), pltpu.roll(below, 3 * SLAB, 1))
    strip = jnp.where(lane < 2 * SLAB, upper, lower)
    rows = 4 * SLAB
    coupling = columns(strip[0:1])[:rows]
    coupling = jnp.concatenate([coupling, coupling], axis=1)
    categories = [columns(strip[1 + block : 2 + block])[:rows] for block in range(2)]

    halo_ref[0, 0:16, :] = jnp.zeros((16, 2 * LB), jnp.float32)
    for g in range(GROUPS):
        at = g * GROUP_ROWS
        for index, reach in enumerate(REACH):
            slab = g * len(REACH) + index
            halo_ref[slab, SLAB - reach : SLAB, :] = above_ref[at : at + reach, :]
            halo_ref[slab, SLAB : SLAB + reach, :] = below_ref[at : at + reach, :]
            at += reach

    def strips(slab, low, high):
        return jnp.concatenate([halo_ref[slab, :SLAB, :], low, high, halo_ref[slab, SLAB:, :]], axis=0)

    starts = [
        strips(g * len(REACH), starts_ref[g, :SLAB, :], starts_ref[g, lines - SLAB :, :]) for g in range(GROUPS)
    ]

    def sources(g, m):
        return strips(
            g * len(REACH) + 1 + m, sources_ref[g, m, :SLAB, :], sources_ref[g, m, lines - SLAB :, :]
        )

    def relaxed_to(g, m, field):
        relaxed_ref[g, m] = field

    out = relaxations(starts, sources, coupling, categories, weights_ref[...], rates_ref, first_ref[0, 0], relaxed_to)
    section = lines + 2 * EDGE
    decay = joined(own_decay_ref[...], out["decay"], EDGE)
    term = joined(own_term_ref[...], out["term"], EDGE)
    for block in range(2):
        at = block * section
        lanes = slice(block * LB, (block + 1) * LB)
        terms_ref[at : at + section, :] = term[:, lanes]
        factors_ref[at : at + section, :] = (decay * decay)[:, lanes]
    shift_ref[...] = joined(own_shift_ref[...], out["shift"], EDGE)
    decay_ref[...] = out["decay"]
    for g in range(GROUPS):
        base_ref[g] = out["bases"][g]
        last_ref[g] = out["lasts"][g]


def scan_kernel(place_ref, terms_ref, factors_ref, entering_ref):
    factor = factors_ref[place_ref[0, 0]]
    carried = jnp.zeros_like(factor)
    for d in range(terms_ref.shape[0]):
        entering_ref[d] = carried
        carried = factor * carried + terms_ref[d]


def final_kernel(
    entering_ref, shift_ref, params_ref, above_ref, below_ref, weights_ref, decay_ref, base_ref, last_ref, relaxed_ref,
    edge_decay_ref, edge_base_ref, edge_last_ref, edge_relaxed_ref, states_hbm, states_ref, sems,
):
    lines = last_ref.shape[1]
    section = lines + 2 * EDGE
    at = GROUPS * GROUP_ROWS

    def along(row):
        own = columns(params_ref[row : row + 1, :])
        above = columns(above_ref[at + row : at + row + 1, :LB])
        below = columns(below_ref[at + row : at + row + 1, :LB])
        return jnp.concatenate([above[lines - EDGE :], own, below[:EDGE]], axis=0)

    coupling = along(0)
    coupling = jnp.concatenate([coupling, coupling], axis=1)
    masks = class_masks([along(1), along(2)])

    entering = jnp.concatenate([entering_ref[:section, :], entering_ref[section:, :]], axis=1)
    shift = shift_ref[...]
    inner = slice(EDGE, EDGE + lines)
    decay = joined(decay_ref[...], edge_decay_ref[...], EDGE)
    base = [joined(base_ref[g], edge_base_ref[g], EDGE) for g in range(GROUPS)]
    last = [joined(last_ref[g], edge_last_ref[g], 0) for g in range(GROUPS)]
    passed = decay * entering

    def send(m):
        copy = pltpu.make_async_copy(states_ref.at[:, m], states_hbm.at[:, m], sems.at[m])
        copy.start()
        return copy

    states_ref[0, 3] = passed[inner] + last[0]
    states_ref[1, 3] = (decay * passed)[inner] + last[1]
    copies = [send(3)]
    state = [entering + shift - base[0], passed + base[1]]
    weights = weights_ref[...]
    for m in range(STEPS - 1):
        state = solve_lines([spread(s, coupling) for s in state], masks, weights)
        for g in range(GROUPS):
            states_ref[g, m] = joined(relaxed_ref[g, m], edge_relaxed_ref[g, m], 0) + state[g][inner]
        copies.append(send(m))
    for copy in copies:
        copy.wait()


def shards(sources, starts, coupling, classes, inverses, coarse_rate):
    count, along = lax.axis_size("tm"), lax.axis_size("space")
    lines, line_len = starts.shape[1:]
    near_rows = lines + 2 * EDGE
    sections = 2 * near_rows
    f32 = jnp.float32
    place = lax.axis_index("tm").astype(jnp.int32).reshape(1, 1)
    first = (lax.axis_index("tm") == 0).astype(jnp.int32).reshape(1, 1)

    def grant(size):
        return pltpu.CompilerParams(vmem_limit_bytes=size * MEBI)

    def shape(*dims):
        return jax.ShapeDtypeStruct(dims, f32)

    message = shape(MESSAGE_ROWS, line_len)
    up, down, params = pl.pallas_call(
        pack_kernel,
        out_shape=(message, message, shape(8, lines)),
        in_specs=[HBM] * 4,
        out_specs=[VMEM] * 3,
        scratch_shapes=[
            pltpu.VMEM((GROUPS, SLAB, line_len), f32),
            pltpu.VMEM((GROUPS, SLAB, line_len), f32),
            pltpu.VMEM((GROUPS, STEPS, SLAB, line_len), f32),
            pltpu.VMEM((GROUPS, STEPS, SLAB, line_len), f32),
            pltpu.VMEM((1, lines), f32),
            pltpu.VMEM((2, lines), jnp.int32),
            pltpu.SemaphoreType.DMA((6,)),
        ],
        compiler_params=grant(4),
        name="pack",
    )(*[
        pltpu.with_memory_space_constraint(x, pltpu.HBM)
        for x in (starts, sources, coupling.reshape(1, lines), classes.T)
    ])

    with jax.named_scope("halo"):
        upward = [(i, i + 1) for i in range(along - 1)]
        above = lax.ppermute(up, "space", upward)
        below = lax.ppermute(down, "space", [(j, i) for i, j in upward])

    with jax.named_scope("weights"):
        transposed = inverses.transpose(0, 2, 1)
        table = jnp.concatenate(
            [
                jnp.concatenate([transposed[0], transposed[2]], axis=1),
                jnp.concatenate([transposed[1], transposed[3]], axis=1),
            ],
            axis=0,
        )
        high = lax.reduce_precision(table, 8, 7)
        weights = jnp.concatenate([high, high, table - high], axis=0).astype(jnp.bfloat16)

    def kept(rows):
        return (
            shape(rows, line_len),
            shape(GROUPS, rows, line_len),
            shape(GROUPS, rows, line_len),
            shape(GROUPS, STEPS - 1, rows, line_len),
        )

    term, shift, *own = pl.pallas_call(
        own_kernel,
        out_shape=(shape(lines, line_len), shape(lines, line_len), *kept(lines)),
        in_specs=[SMEM] + [VMEM] * 5,
        out_specs=[VMEM] * 6,
        compiler_params=grant(24),
        cost_estimate=pl.CostEstimate(flops=5_000_000_000, bytes_accessed=4_000_000, transcendentals=0),
        name="own",
    )(first, starts, sources, params, weights, coarse_rate)
    terms, factors, shift, *edges = pl.pallas_call(
        edge_kernel,
        out_shape=(shape(sections, LB), shape(sections, LB), shape(near_rows, line_len), *kept(4 * SLAB)),
        in_specs=[SMEM] + [VMEM] * 10,
        out_specs=[VMEM] * 7,
        scratch_shapes=[pltpu.VMEM((GROUPS * len(REACH), 2 * SLAB, line_len), f32)],
        compiler_params=grant(20),
        name="edge",
    )(first, starts, sources, params, above, below, weights, coarse_rate, term, shift, own[0])

    split = (count, 1, sections * LB // count)
    with jax.named_scope("onward"):
        shift = lax.ppermute(shift, "tm", [(i, i + 1) for i in range(count - 1)])
    with jax.named_scope("gather_terms"):
        terms = lax.all_to_all(terms.reshape(split), "tm", 0, 0)
    entering = pl.pallas_call(
        scan_kernel,
        out_shape=shape(*split),
        in_specs=[SMEM] + [VMEM] * 2,
        out_specs=VMEM,
        compiler_params=grant(4),
        name="scan",
    )(place, terms, factors.reshape(split))
    with jax.named_scope("return_terms"):
        entering = lax.all_to_all(entering, "tm", 0, 0)
    return pl.pallas_call(
        final_kernel,
        out_shape=shape(GROUPS, STEPS, lines, line_len),
        in_specs=[VMEM] * 14,
        out_specs=HBM,
        scratch_shapes=[
            pltpu.VMEM((GROUPS, STEPS, lines, line_len), f32),
            pltpu.SemaphoreType.DMA((STEPS,)),
        ],
        compiler_params=grant(20),
        name="final",
    )(entering.reshape(sections, LB), shift, params, above, below, weights, *own, *edges)


def solution(mesh):
    in_specs = (
        P("tm", None, "space", None),
        P("tm", "space", None),
        P("space"),
        P("space", None),
        P(),
        P(),
    )
    out_specs = P("tm", None, "space", None)
    return jax.shard_map(shards, mesh=mesh, in_specs=in_specs, out_specs=out_specs, check_vma=False)
```

```python
import functools

import jax
import jax.numpy as jnp
from jax import lax
from jax.experimental import pallas as pl
from jax.experimental.pallas import tpu as pltpu
from jax.sharding import PartitionSpec as P

LB = 128
GROUPS = 2
STEPS = 4
SLAB = 16
EDGE = 8
REACH = (11, 10, 9, 8, 7)
GROUP_ROWS = sum(REACH)
MESSAGE_ROWS = 96
VMEM = pl.BlockSpec(memory_space=pltpu.VMEM)
SMEM = pl.BlockSpec(memory_space=pltpu.SMEM)
HBM = pl.BlockSpec(memory_space=pltpu.HBM)
MEBI = 1024 * 1024


def columns(row):
    return jnp.broadcast_to(row, (LB, LB)).T


def class_masks(categories):
    even, odd, upper = [], [], []
    for category in categories:
        high = category > 1.5
        low = category - jnp.where(high, 2.0, 0.0)
        odd.append(jnp.where(low > 0.5, 1.0, 0.0).astype(jnp.bfloat16))
        even.append(jnp.where(low > 0.5, 0.0, 1.0).astype(jnp.bfloat16))
        upper.append(high)
    return even, odd, upper


def rates_of(categories, rates_ref):
    blocks = []
    for category in categories:
        rate = jnp.broadcast_to(rates_ref[0:1, :], category.shape)
        for c in range(1, 4):
            rate = jnp.where(category > c - 0.5, jnp.broadcast_to(rates_ref[c : c + 1, :], category.shape), rate)
        blocks.append(rate)
    return jnp.concatenate(blocks, axis=1)


def solve_field(field, masks, weights):
    even, odd, upper = masks
    rows = field.shape[0]
    left = []
    for block in range(2):
        x = field[:, block * LB : (block + 1) * LB]
        high = x.astype(jnp.bfloat16)
        low = (x - high.astype(jnp.float32)).astype(jnp.bfloat16)
        high_pair = [high * even[block], high * odd[block]]
        low_pair = [low * even[block], low * odd[block]]
        left.append(jnp.concatenate(high_pair + low_pair + high_pair, axis=1))
    product = jnp.dot(jnp.concatenate(left, axis=0), weights, preferred_element_type=jnp.float32)
    blocks = []
    for block in range(2):
        part = product[block * rows : (block + 1) * rows]
        blocks.append(jnp.where(upper[block], part[:, LB:], part[:, :LB]))
    return jnp.concatenate(blocks, axis=1)


def solve_lines(fields, masks, weights):
    return [solve_field(field, masks, weights) for field in fields]


def spread(field, coupling):
    rows = field.shape[0]
    return field + coupling * (pltpu.roll(field, 1, 0) + pltpu.roll(field, rows - 1, 0))


def relaxations(starts, sources, coupling, categories, weights, rates_ref, first, relaxed_to):
    masks = class_masks(categories)
    linear, state = starts[0], starts
    for m in range(STEPS):
        *state, linear = solve_lines(
            [spread(state[g], coupling) + sources(g, m) for g in range(GROUPS)] + [spread(linear, coupling)],
            masks,
            weights,
        )
        if m < STEPS - 1:
            for g in range(GROUPS):
                relaxed_to(g, m, state[g])
    ends = state
    linear = jnp.where(first > 0, jnp.zeros_like(linear), linear)
    change = ends[0] - starts[1]
    resid, onward = change, ends[1]
    for m in range(STEPS):
        resid, onward = solve_lines([spread(resid, coupling), spread(onward, coupling)], masks, weights)
    rates = rates_of(categories, rates_ref)
    decay = jnp.exp(-rates)
    ahead = onward * jnp.exp(rates)
    held = decay * linear
    return dict(
        term=resid + ahead - held,
        shift=ends[1] - ahead,
        decay=decay,
        bases=(jnp.where(first > 0, jnp.zeros_like(linear), starts[0]), change - linear),
        lasts=(ends[0] - linear, ends[1] + resid - held),
    )


def pack_kernel(
    starts_hbm, sources_hbm, coupling_hbm, classes_hbm, up_ref, down_ref, params_ref, starts_ref, sources_ref,
    starts_low, starts_high, sources_low, sources_high, coupling_row, classes_rows, sems,
):
    lines = starts_hbm.shape[1]
    low, high = pl.ds(0, SLAB), pl.ds(lines - SLAB, SLAB)
    pairs = [
        (sources_hbm.at[:, :, high, :], sources_high),
        (sources_hbm.at[:, :, low, :], sources_low),
        (starts_hbm.at[:, high, :], starts_high),
        (starts_hbm.at[:, low, :], starts_low),
        (coupling_hbm, coupling_row),
        (classes_hbm, classes_rows),
        (starts_hbm, starts_ref),
        (sources_hbm, sources_ref),
    ]
    whole = 2
    copies = [pltpu.make_async_copy(src, dst, sems.at[i]) for i, (src, dst) in enumerate(pairs)]
    for copy in copies:
        copy.start()
    for ref in (up_ref, down_ref, params_ref):
        ref[...] = jnp.zeros_like(ref)
    for copy in copies[:-whole]:
        copy.wait()
    params_ref[0:1, :] = coupling_row[...]
    params_ref[1:3, :] = classes_rows[...].astype(jnp.float32)
    for g in range(GROUPS):
        at = g * GROUP_ROWS
        for index, reach in enumerate(REACH):
            if index == 0:
                up, down = starts_high[g, SLAB - reach :, :], starts_low[g, :reach, :]
            else:
                up, down = sources_high[g, index - 1, SLAB - reach :, :], sources_low[g, index - 1, :reach, :]
            up_ref[at : at + reach, :] = up
            down_ref[at : at + reach, :] = down
            at += reach
    for ref in (up_ref, down_ref):
        ref[GROUPS * GROUP_ROWS : GROUPS * GROUP_ROWS + 3, :LB] = params_ref[0:3, :]
    for copy in copies[-whole:]:
        copy.wait()


def own_kernel(
    first_ref, starts_ref, sources_ref, params_ref, weights_ref, rates_ref,
    term_ref, shift_ref, decay_ref, base_ref, last_ref, relaxed_ref,
):
    coupling = columns(params_ref[0:1, :])
    coupling = jnp.concatenate([coupling, coupling], axis=1)
    categories = [columns(params_ref[1 + block : 2 + block, :]) for block in range(2)]

    def relaxed_to(g, m, field):
        relaxed_ref[g, m] = field

    out = relaxations(
        [starts_ref[g] for g in range(GROUPS)], lambda g, m: sources_ref[g, m], coupling, categories, weights_ref[...],
        rates_ref, first_ref[0, 0], relaxed_to,
    )
    term_ref[...] = out["term"]
    shift_ref[...] = out["shift"]
    decay_ref[...] = out["decay"]
    for g in range(GROUPS):
        base_ref[g] = out["bases"][g]
        last_ref[g] = out["lasts"][g]


def joined(inner, strip, beyond):
    lines = inner.shape[0]
    return jnp.concatenate([strip[16 - beyond : 24], inner[EDGE : lines - EDGE], strip[40 : 48 + beyond]], axis=0)


def edge_kernel(
    first_ref, starts_ref, sources_ref, params_ref, above_ref, below_ref, weights_ref, rates_ref,
    own_term_ref, own_shift_ref, own_decay_ref,
    terms_ref, factors_ref, shift_ref, decay_ref, base_ref, last_ref, relaxed_ref, halo_ref,
):
    lines = starts_ref.shape[1]
    lane = lax.broadcasted_iota(jnp.int32, (8, LB), 1)
    at = GROUPS * GROUP_ROWS
    own = params_ref[...]
    halo_ref[...] = jnp.zeros_like(halo_ref)
    halo_ref[0, 0:3, :LB] = above_ref[at : at + 3, :LB]
    halo_ref[0, 8:11, :LB] = below_ref[at : at + 3, :LB]
    above, below = halo_ref[0, 0:8, :LB], halo_ref[0, 8:16, :LB]
    upper = jnp.where(lane < SLAB, pltpu.roll(above, SLAB, 1), pltpu.roll(own, SLAB, 1))
    lower = jnp.where(lane < 3 * SLAB, pltpu.roll(own, 3 * SLAB, 1), pltpu.roll(below, 3 * SLAB, 1))
    strip = jnp.where(lane < 2 * SLAB, upper, lower)
    rows = 4 * SLAB
    coupling = columns(strip[0:1])[:rows]
    coupling = jnp.concatenate([coupling, coupling], axis=1)
    categories = [columns(strip[1 + block : 2 + block])[:rows] for block in range(2)]

    halo_ref[0, 0:16, :] = jnp.zeros((16, 2 * LB), jnp.float32)
    for g in range(GROUPS):
        at = g * GROUP_ROWS
        for index, reach in enumerate(REACH):
            slab = g * len(REACH) + index
            halo_ref[slab, SLAB - reach : SLAB, :] = above_ref[at : at + reach, :]
            halo_ref[slab, SLAB : SLAB + reach, :] = below_ref[at : at + reach, :]
            at += reach

    def strips(slab, low, high):
        return jnp.concatenate([halo_ref[slab, :SLAB, :], low, high, halo_ref[slab, SLAB:, :]], axis=0)

    starts = [
        strips(g * len(REACH), starts_ref[g, :SLAB, :], starts_ref[g, lines - SLAB :, :]) for g in range(GROUPS)
    ]

    def sources(g, m):
        return strips(
            g * len(REACH) + 1 + m, sources_ref[g, m, :SLAB, :], sources_ref[g, m, lines - SLAB :, :]
        )

    def relaxed_to(g, m, field):
        relaxed_ref[g, m] = field

    out = relaxations(starts, sources, coupling, categories, weights_ref[...], rates_ref, first_ref[0, 0], relaxed_to)
    section = lines + 2 * EDGE
    decay = joined(own_decay_ref[...], out["decay"], EDGE)
    term = joined(own_term_ref[...], out["term"], EDGE)
    for block in range(2):
        at = block * section
        lanes = slice(block * LB, (block + 1) * LB)
        terms_ref[at : at + section, :] = term[:, lanes]
        factors_ref[at : at + section, :] = (decay * decay)[:, lanes]
    shift_ref[...] = joined(own_shift_ref[...], out["shift"], EDGE)
    decay_ref[...] = out["decay"]
    for g in range(GROUPS):
        base_ref[g] = out["bases"][g]
        last_ref[g] = out["lasts"][g]


def scan_kernel(place_ref, terms_ref, factors_ref, entering_ref):
    factor = factors_ref[place_ref[0, 0]]
    carried = jnp.zeros_like(factor)
    for d in range(terms_ref.shape[0]):
        entering_ref[d] = carried
        carried = factor * carried + terms_ref[d]


def final_kernel(
    entering_ref, shift_ref, params_ref, above_ref, below_ref, weights_ref, decay_ref, base_ref, last_ref, relaxed_ref,
    edge_decay_ref, edge_base_ref, edge_last_ref, edge_relaxed_ref, states_hbm, states_ref, sems,
):
    lines = last_ref.shape[1]
    section = lines + 2 * EDGE
    at = GROUPS * GROUP_ROWS

    def along(row):
        own = columns(params_ref[row : row + 1, :])
        above = columns(above_ref[at + row : at + row + 1, :LB])
        below = columns(below_ref[at + row : at + row + 1, :LB])
        return jnp.concatenate([above[lines - EDGE :], own, below[:EDGE]], axis=0)

    coupling = along(0)
    coupling = jnp.concatenate([coupling, coupling], axis=1)
    masks = class_masks([along(1), along(2)])

    entering = jnp.concatenate([entering_ref[:section, :], entering_ref[section:, :]], axis=1)
    shift = shift_ref[...]
    inner = slice(EDGE, EDGE + lines)
    decay = joined(decay_ref[...], edge_decay_ref[...], EDGE)
    base = [joined(base_ref[g], edge_base_ref[g], EDGE) for g in range(GROUPS)]
    last = [joined(last_ref[g], edge_last_ref[g], 0) for g in range(GROUPS)]
    passed = decay * entering

    def send(m):
        copy = pltpu.make_async_copy(states_ref.at[:, m], states_hbm.at[:, m], sems.at[m])
        copy.start()
        return copy

    states_ref[0, 3] = passed[inner] + last[0]
    states_ref[1, 3] = (decay * passed)[inner] + last[1]
    copies = [send(3)]
    state = [entering + shift - base[0], passed + base[1]]
    weights = weights_ref[...]
    for m in range(STEPS - 1):
        state = solve_lines([spread(s, coupling) for s in state], masks, weights)
        for g in range(GROUPS):
            states_ref[g, m] = joined(relaxed_ref[g, m], edge_relaxed_ref[g, m], 0) + state[g][inner]
        copies.append(send(m))
    for copy in copies:
        copy.wait()


def shards(sources, starts, coupling, classes, inverses, coarse_rate):
    count, along = lax.axis_size("tm"), lax.axis_size("space")
    lines, line_len = starts.shape[1:]
    near_rows = lines + 2 * EDGE
    sections = 2 * near_rows
    f32 = jnp.float32
    place = lax.axis_index("tm").astype(jnp.int32).reshape(1, 1)
    first = (lax.axis_index("tm") == 0).astype(jnp.int32).reshape(1, 1)

    def grant(size):
        return pltpu.CompilerParams(vmem_limit_bytes=size * MEBI)

    def shape(*dims):
        return jax.ShapeDtypeStruct(dims, f32)

    message = shape(MESSAGE_ROWS, line_len)
    up, down, params, held_starts, held_sources = pl.pallas_call(
        pack_kernel,
        out_shape=(message, message, shape(8, lines), shape(*starts.shape), shape(*sources.shape)),
        in_specs=[HBM] * 4,
        out_specs=[VMEM] * 5,
        scratch_shapes=[
            pltpu.VMEM((GROUPS, SLAB, line_len), f32),
            pltpu.VMEM((GROUPS, SLAB, line_len), f32),
            pltpu.VMEM((GROUPS, STEPS, SLAB, line_len), f32),
            pltpu.VMEM((GROUPS, STEPS, SLAB, line_len), f32),
            pltpu.VMEM((1, lines), f32),
            pltpu.VMEM((2, lines), jnp.int32),
            pltpu.SemaphoreType.DMA((8,)),
        ],
        compiler_params=grant(6),
        name="pack",
    )(*[
        pltpu.with_memory_space_constraint(x, pltpu.HBM)
        for x in (starts, sources, coupling.reshape(1, lines), classes.T)
    ])

    with jax.named_scope("halo"):
        upward = [(i, i + 1) for i in range(along - 1)]
        above = lax.ppermute(up, "space", upward)
        below = lax.ppermute(down, "space", [(j, i) for i, j in upward])

    with jax.named_scope("weights"):
        transposed = inverses.transpose(0, 2, 1)
        table = jnp.concatenate(
            [
                jnp.concatenate([transposed[0], transposed[2]], axis=1),
                jnp.concatenate([transposed[1], transposed[3]], axis=1),
            ],
            axis=0,
        )
        high = lax.reduce_precision(table, 8, 7)
        weights = jnp.concatenate([high, high, table - high], axis=0).astype(jnp.bfloat16)

    def kept(rows):
        return (
            shape(rows, line_len),
            shape(GROUPS, rows, line_len),
            shape(GROUPS, rows, line_len),
            shape(GROUPS, STEPS - 1, rows, line_len),
        )

    term, shift, *own = pl.pallas_call(
        own_kernel,
        out_shape=(shape(lines, line_len), shape(lines, line_len), *kept(lines)),
        in_specs=[SMEM] + [VMEM] * 5,
        out_specs=[VMEM] * 6,
        compiler_params=grant(24),
        cost_estimate=pl.CostEstimate(flops=5_000_000_000, bytes_accessed=4_000_000, transcendentals=0),
        name="own",
    )(first, held_starts, held_sources, params, weights, coarse_rate)
    terms, factors, shift, *edges = pl.pallas_call(
        edge_kernel,
        out_shape=(shape(sections, LB), shape(sections, LB), shape(near_rows, line_len), *kept(4 * SLAB)),
        in_specs=[SMEM] + [VMEM] * 10,
        out_specs=[VMEM] * 7,
        scratch_shapes=[pltpu.VMEM((GROUPS * len(REACH), 2 * SLAB, line_len), f32)],
        compiler_params=grant(20),
        name="edge",
    )(first, held_starts, held_sources, params, above, below, weights, coarse_rate, term, shift, own[0])

    split = (count, 1, sections * LB // count)
    with jax.named_scope("onward"):
        shift = lax.ppermute(shift, "tm", [(i, i + 1) for i in range(count - 1)])
    with jax.named_scope("gather_terms"):
        terms = lax.all_to_all(terms.reshape(split), "tm", 0, 0)
    entering = pl.pallas_call(
        scan_kernel,
        out_shape=pltpu.VMEM(split, f32),
        in_specs=[SMEM] + [VMEM] * 2,
        out_specs=VMEM,
        compiler_params=grant(4),
        name="scan",
    )(place, terms, factors.reshape(split))
    with jax.named_scope("return_terms"):
        entering = lax.all_to_all(entering, "tm", 0, 0)
    return pl.pallas_call(
        final_kernel,
        out_shape=shape(GROUPS, STEPS, lines, line_len),
        in_specs=[VMEM] * 14,
        out_specs=HBM,
        scratch_shapes=[
            pltpu.VMEM((GROUPS, STEPS, lines, line_len), f32),
            pltpu.SemaphoreType.DMA((STEPS,)),
        ],
        compiler_params=grant(20),
        name="final",
    )(entering.reshape(sections, LB), shift, params, above, below, weights, *own, *edges)


def solution(mesh):
    in_specs = (
        P("tm", None, "space", None),
        P("tm", "space", None),
        P("space"),
        P("space", None),
        P(),
        P(),
    )
    out_specs = P("tm", None, "space", None)
    return jax.shard_map(shards, mesh=mesh, in_specs=in_specs, out_specs=out_specs, check_vma=False)
```

```python
import functools

import jax
import jax.numpy as jnp
from jax import lax
from jax.experimental import pallas as pl
from jax.experimental.pallas import tpu as pltpu
from jax.sharding import PartitionSpec as P

LB = 128
GROUPS = 2
STEPS = 4
SLAB = 16
EDGE = 8
REACH = (11, 10, 9, 8, 7)
GROUP_ROWS = sum(REACH)
MESSAGE_ROWS = 96
VMEM = pl.BlockSpec(memory_space=pltpu.VMEM)
SMEM = pl.BlockSpec(memory_space=pltpu.SMEM)
HBM = pl.BlockSpec(memory_space=pltpu.HBM)
MEBI = 1024 * 1024


def columns(row):
    return jnp.broadcast_to(row, (LB, LB)).T


def class_masks(categories):
    even, odd, upper = [], [], []
    for category in categories:
        high = category > 1.5
        low = category - jnp.where(high, 2.0, 0.0)
        odd.append(jnp.where(low > 0.5, 1.0, 0.0).astype(jnp.bfloat16))
        even.append(jnp.where(low > 0.5, 0.0, 1.0).astype(jnp.bfloat16))
        upper.append(high)
    return even, odd, upper


def rates_of(categories, rates_ref):
    blocks = []
    for category in categories:
        rate = jnp.broadcast_to(rates_ref[0:1, :], category.shape)
        for c in range(1, 4):
            rate = jnp.where(category > c - 0.5, jnp.broadcast_to(rates_ref[c : c + 1, :], category.shape), rate)
        blocks.append(rate)
    return jnp.concatenate(blocks, axis=1)


def solve_field(field, masks, weights):
    even, odd, upper = masks
    rows = field.shape[0]
    left = []
    for block in range(2):
        x = field[:, block * LB : (block + 1) * LB]
        high = x.astype(jnp.bfloat16)
        low = (x - high.astype(jnp.float32)).astype(jnp.bfloat16)
        high_pair = [high * even[block], high * odd[block]]
        low_pair = [low * even[block], low * odd[block]]
        left.append(jnp.concatenate(high_pair + low_pair + high_pair, axis=1))
    product = jnp.dot(jnp.concatenate(left, axis=0), weights, preferred_element_type=jnp.float32)
    blocks = []
    for block in range(2):
        part = product[block * rows : (block + 1) * rows]
        blocks.append(jnp.where(upper[block], part[:, LB:], part[:, :LB]))
    return jnp.concatenate(blocks, axis=1)


def solve_lines(fields, masks, weights):
    return [solve_field(field, masks, weights) for field in fields]


def spread(field, coupling):
    rows = field.shape[0]
    return field + coupling * (pltpu.roll(field, 1, 0) + pltpu.roll(field, rows - 1, 0))


def relaxations(starts, sources, coupling, categories, weights, rates_ref, first, relaxed_to):
    masks = class_masks(categories)
    linear, state = starts[0], starts
    for m in range(STEPS):
        *state, linear = solve_lines(
            [spread(state[g], coupling) + sources(g, m) for g in range(GROUPS)] + [spread(linear, coupling)],
            masks,
            weights,
        )
        if m < STEPS - 1:
            for g in range(GROUPS):
                relaxed_to(g, m, state[g])
    ends = state
    linear = jnp.where(first > 0, jnp.zeros_like(linear), linear)
    change = ends[0] - starts[1]
    resid, onward = change, ends[1]
    for m in range(STEPS):
        resid, onward = solve_lines([spread(resid, coupling), spread(onward, coupling)], masks, weights)
    rates = rates_of(categories, rates_ref)
    decay = jnp.exp(-rates)
    ahead = onward * jnp.exp(rates)
    held = decay * linear
    return dict(
        term=resid + ahead - held,
        shift=ends[1] - ahead,
        decay=decay,
        bases=(jnp.where(first > 0, jnp.zeros_like(linear), starts[0]), change - linear),
        lasts=(ends[0] - linear, ends[1] + resid - held),
    )


def pack_kernel(
    starts_hbm, sources_hbm, coupling_hbm, classes_hbm, rates_hbm,
    up_ref, down_ref, params_ref, rates_ref, starts_ref, starts_low, starts_high, sources_low, sources_high,
    coupling_row, classes_rows, sems,
):
    lines = starts_hbm.shape[1]
    low, high = pl.ds(0, SLAB), pl.ds(lines - SLAB, SLAB)
    pairs = [
        (sources_hbm.at[:, :, high, :], sources_high),
        (sources_hbm.at[:, :, low, :], sources_low),
        (starts_hbm.at[:, high, :], starts_high),
        (starts_hbm.at[:, low, :], starts_low),
        (coupling_hbm, coupling_row),
        (classes_hbm, classes_rows),
        (starts_hbm, starts_ref),
        (rates_hbm, rates_ref),
    ]
    whole = 2
    copies = [pltpu.make_async_copy(src, dst, sems.at[i]) for i, (src, dst) in enumerate(pairs)]
    for copy in copies:
        copy.start()
    for ref in (up_ref, down_ref, params_ref):
        ref[...] = jnp.zeros_like(ref)
    for copy in copies[:-whole]:
        copy.wait()
    params_ref[0:1, :] = coupling_row[...]
    params_ref[1:3, :] = classes_rows[...].astype(jnp.float32)
    for g in range(GROUPS):
        at = g * GROUP_ROWS
        for index, reach in enumerate(REACH):
            if index == 0:
                up, down = starts_high[g, SLAB - reach :, :], starts_low[g, :reach, :]
            else:
                up, down = sources_high[g, index - 1, SLAB - reach :, :], sources_low[g, index - 1, :reach, :]
            up_ref[at : at + reach, :] = up
            down_ref[at : at + reach, :] = down
            at += reach
    for ref in (up_ref, down_ref):
        ref[GROUPS * GROUP_ROWS : GROUPS * GROUP_ROWS + 3, :LB] = params_ref[0:3, :]
    for copy in copies[-whole:]:
        copy.wait()


def own_kernel(
    first_ref, sources_hbm, starts_ref, params_ref, weights_ref, rates_ref,
    term_ref, shift_ref, decay_ref, base_ref, last_ref, lines_ref, relaxed_hbm,
    sources_ref, relaxed_ref, in_sems, out_sems,
):
    arriving = [
        pltpu.make_async_copy(sources_hbm.at[:, m], sources_ref.at[:, m], in_sems.at[m]) for m in range(STEPS)
    ]
    for copy in arriving:
        copy.start()
    coupling, *categories = [columns(params_ref[row : row + 1, :]) for row in range(3)]
    for row, values in enumerate([coupling, *categories]):
        lines_ref[row] = values
    coupling = jnp.concatenate([coupling, coupling], axis=1)

    leaving = []

    def sources(g, m):
        if g == 0:
            arriving[m].wait()
        return sources_ref[g, m]

    def relaxed_to(g, m, field):
        relaxed_ref[g, m] = field
        if g == GROUPS - 1:
            leaving.append(pltpu.make_async_copy(relaxed_ref.at[:, m], relaxed_hbm.at[:, m], out_sems.at[m]))
            leaving[-1].start()

    out = relaxations(
        [starts_ref[g] for g in range(GROUPS)], sources, coupling, categories, weights_ref[...], rates_ref,
        first_ref[0, 0], relaxed_to,
    )
    term_ref[...] = out["term"]
    shift_ref[...] = out["shift"]
    decay_ref[...] = out["decay"]
    for g in range(GROUPS):
        base_ref[g] = out["bases"][g]
        last_ref[g] = out["lasts"][g]
    for copy in leaving:
        copy.wait()


def ends_of(strip, beyond):
    return jnp.concatenate([strip[16 - beyond : 24], strip[40 : 48 + beyond]], axis=0)


def joined(inner, ends):
    lines, half = inner.shape[0], ends.shape[0] // 2
    return jnp.concatenate([ends[:half], inner[EDGE : lines - EDGE], ends[half:]], axis=0)


def edge_kernel(
    first_ref, starts_low, starts_high, sources_low, sources_high, params_ref, above_ref, below_ref, weights_ref,
    rates_ref, own_term_ref, own_shift_ref, own_decay_ref,
    terms_ref, factors_ref, shift_ref, decay_ref, base_ref, last_ref, lines_ref, relaxed_ref, halo_ref,
):
    lines = params_ref.shape[1]
    lane = lax.broadcasted_iota(jnp.int32, (8, LB), 1)
    at = GROUPS * GROUP_ROWS
    own = params_ref[...]
    halo_ref[...] = jnp.zeros_like(halo_ref)
    halo_ref[0, 0:3, :LB] = above_ref[at : at + 3, :LB]
    halo_ref[0, 8:11, :LB] = below_ref[at : at + 3, :LB]
    above, below = halo_ref[0, 0:8, :LB], halo_ref[0, 8:16, :LB]
    upper = jnp.where(lane < SLAB, pltpu.roll(above, SLAB, 1), pltpu.roll(own, SLAB, 1))
    lower = jnp.where(lane < 3 * SLAB, pltpu.roll(own, 3 * SLAB, 1), pltpu.roll(below, 3 * SLAB, 1))
    strip = jnp.where(lane < 2 * SLAB, upper, lower)
    rows = 4 * SLAB
    coupling, *categories = [columns(strip[row : row + 1])[:rows] for row in range(3)]
    for row, values in enumerate([coupling, *categories]):
        lines_ref[row] = ends_of(values, EDGE)
    coupling = jnp.concatenate([coupling, coupling], axis=1)

    halo_ref[0, 0:16, :] = jnp.zeros((16, 2 * LB), jnp.float32)
    for g in range(GROUPS):
        at = g * GROUP_ROWS
        for index, reach in enumerate(REACH):
            slab = g * len(REACH) + index
            halo_ref[slab, SLAB - reach : SLAB, :] = above_ref[at : at + reach, :]
            halo_ref[slab, SLAB : SLAB + reach, :] = below_ref[at : at + reach, :]
            at += reach

    def strips(slab, low, high):
        return jnp.concatenate([halo_ref[slab, :SLAB, :], low, high, halo_ref[slab, SLAB:, :]], axis=0)

    starts = [strips(g * len(REACH), starts_low[g], starts_high[g]) for g in range(GROUPS)]

    def sources(g, m):
        return strips(g * len(REACH) + 1 + m, sources_low[g, m], sources_high[g, m])

    def relaxed_to(g, m, field):
        relaxed_ref[g, m] = ends_of(field, 0)

    out = relaxations(starts, sources, coupling, categories, weights_ref[...], rates_ref, first_ref[0, 0], relaxed_to)
    section = lines + 2 * EDGE
    end_decay = ends_of(out["decay"], EDGE)
    decay = joined(own_decay_ref[...], end_decay)
    term = joined(own_term_ref[...], ends_of(out["term"], EDGE))
    for block in range(2):
        at = block * section
        lanes = slice(block * LB, (block + 1) * LB)
        terms_ref[at : at + section, :] = term[:, lanes]
        factors_ref[at : at + section, :] = (decay * decay)[:, lanes]
    shift_ref[...] = joined(own_shift_ref[...], ends_of(out["shift"], EDGE))
    decay_ref[...] = end_decay
    for g in range(GROUPS):
        base_ref[g] = ends_of(out["bases"][g], EDGE)
        last_ref[g] = ends_of(out["lasts"][g], 0)


def scan_kernel(place_ref, terms_ref, factors_ref, shift_ref, entering_ref):
    del shift_ref
    factor = factors_ref[place_ref[0, 0]]
    carried = jnp.zeros_like(factor)
    for d in range(terms_ref.shape[0]):
        entering_ref[d] = carried
        carried = factor * carried + terms_ref[d]


def final_kernel(
    entering_ref, shift_ref, weights_ref, decay_ref, base_ref, last_ref, lines_ref, relaxed_hbm,
    edge_decay_ref, edge_base_ref, edge_last_ref, edge_lines_ref, edge_relaxed_ref,
    states_hbm, states_ref, relaxed_ref, sems, in_sem,
):
    lines = last_ref.shape[1]
    section = lines + 2 * EDGE
    arriving = pltpu.make_async_copy(relaxed_hbm, relaxed_ref, in_sem)
    arriving.start()
    coupling, *categories = [joined(lines_ref[row], edge_lines_ref[row]) for row in range(3)]
    coupling = jnp.concatenate([coupling, coupling], axis=1)
    masks = class_masks(categories)

    entering = jnp.concatenate([entering_ref[:section, :], entering_ref[section:, :]], axis=1)
    shift = shift_ref[...]
    inner = slice(EDGE, EDGE + lines)
    decay = joined(decay_ref[...], edge_decay_ref[...])
    base = [joined(base_ref[g], edge_base_ref[g]) for g in range(GROUPS)]
    last = [joined(last_ref[g], edge_last_ref[g]) for g in range(GROUPS)]
    passed = decay * entering

    def send(m):
        copy = pltpu.make_async_copy(states_ref.at[:, m], states_hbm.at[:, m], sems.at[m])
        copy.start()
        return copy

    states_ref[0, 3] = passed[inner] + last[0]
    states_ref[1, 3] = (decay * passed)[inner] + last[1]
    copies = [send(3)]
    state = [entering + shift - base[0], passed + base[1]]
    weights = weights_ref[...]
    for m in range(STEPS - 1):
        state = solve_lines([spread(s, coupling) for s in state], masks, weights)
        if m == 0:
            arriving.wait()
        for g in range(GROUPS):
            states_ref[g, m] = joined(relaxed_ref[g, m], edge_relaxed_ref[g, m]) + state[g][inner]
        copies.append(send(m))
    for copy in copies:
        copy.wait()


def shards(sources, starts, coupling, classes, inverses, coarse_rate):
    count, along = lax.axis_size("tm"), lax.axis_size("space")
    lines, line_len = starts.shape[1:]
    near_rows = lines + 2 * EDGE
    sections = 2 * near_rows
    f32 = jnp.float32
    place = lax.axis_index("tm").astype(jnp.int32).reshape(1, 1)
    first = (lax.axis_index("tm") == 0).astype(jnp.int32).reshape(1, 1)

    def grant(size):
        return pltpu.CompilerParams(vmem_limit_bytes=size * MEBI)

    def in_hbm(x):
        return pltpu.with_memory_space_constraint(x, pltpu.HBM)

    def shape(*dims):
        return jax.ShapeDtypeStruct(dims, f32)

    message = shape(MESSAGE_ROWS, line_len)
    up, down, params, rates, held_starts, *slabs = pl.pallas_call(
        pack_kernel,
        out_shape=(
            message,
            message,
            shape(8, lines),
            shape(*coarse_rate.shape),
            shape(*starts.shape),
            shape(GROUPS, SLAB, line_len),
            shape(GROUPS, SLAB, line_len),
            shape(GROUPS, STEPS, SLAB, line_len),
            shape(GROUPS, STEPS, SLAB, line_len),
        ),
        in_specs=[HBM] * 5,
        out_specs=[VMEM] * 9,
        scratch_shapes=[
            pltpu.VMEM((1, lines), f32),
            pltpu.VMEM((2, lines), jnp.int32),
            pltpu.SemaphoreType.DMA((8,)),
        ],
        compiler_params=grant(6),
        name="pack",
    )(*[
        in_hbm(x)
        for x in (starts, sources, coupling.reshape(1, lines), classes.T, coarse_rate)
    ])

    with jax.named_scope("halo"):
        upward = [(i, i + 1) for i in range(along - 1)]
        above = lax.ppermute(up, "space", upward)
        below = lax.ppermute(down, "space", [(j, i) for i, j in upward])

    with jax.named_scope("weights"):
        transposed = inverses.transpose(0, 2, 1)
        table = jnp.concatenate(
            [
                jnp.concatenate([transposed[0], transposed[2]], axis=1),
                jnp.concatenate([transposed[1], transposed[3]], axis=1),
            ],
            axis=0,
        )
        high = lax.reduce_precision(table, 8, 7)
        weights = jnp.concatenate([high, high, table - high], axis=0).astype(jnp.bfloat16)

    def kept(rows, wide_rows):
        return (
            shape(wide_rows, line_len),
            shape(GROUPS, wide_rows, line_len),
            shape(GROUPS, rows, line_len),
            shape(3, wide_rows, LB),
            shape(GROUPS, STEPS - 1, rows, line_len),
        )

    held = pltpu.VMEM((GROUPS, STEPS - 1, lines, line_len), f32)
    term, shift, *own = pl.pallas_call(
        own_kernel,
        out_shape=(
            shape(lines, line_len),
            shape(lines, line_len),
            *kept(lines, lines)[:-1],
            pltpu.HBM((GROUPS, STEPS - 1, lines, line_len), f32),
        ),
        in_specs=[SMEM, HBM] + [VMEM] * 4,
        out_specs=[VMEM] * 6 + [HBM],
        scratch_shapes=[
            pltpu.VMEM((GROUPS, STEPS, lines, line_len), f32),
            held,
            pltpu.SemaphoreType.DMA((STEPS,)),
            pltpu.SemaphoreType.DMA((STEPS - 1,)),
        ],
        compiler_params=grant(24),
        cost_estimate=pl.CostEstimate(flops=5_000_000_000, bytes_accessed=4_000_000, transcendentals=0),
        name="own",
    )(first, in_hbm(sources), held_starts, params, weights, rates)
    terms, factors, shift, *edges = pl.pallas_call(
        edge_kernel,
        out_shape=(
            shape(sections, LB),
            shape(sections, LB),
            shape(near_rows, line_len),
            *kept(2 * EDGE, 4 * EDGE),
        ),
        in_specs=[SMEM] + [VMEM] * 12,
        out_specs=[VMEM] * 8,
        scratch_shapes=[pltpu.VMEM((GROUPS * len(REACH), 2 * SLAB, line_len), f32)],
        compiler_params=grant(20),
        name="edge",
    )(first, *slabs, params, above, below, weights, rates, term, shift, own[0])

    split = (count, 1, sections * LB // count)
    with jax.named_scope("onward"):
        shift = lax.ppermute(shift, "tm", [(i, i + 1) for i in range(count - 1)])
    with jax.named_scope("gather_terms"):
        terms = lax.all_to_all(terms.reshape(split), "tm", 0, 0)
    entering = pl.pallas_call(
        scan_kernel,
        out_shape=shape(*split),
        in_specs=[SMEM] + [VMEM] * 3,
        out_specs=VMEM,
        compiler_params=grant(4),
        name="scan",
    )(place, terms, factors.reshape(split), shift)
    with jax.named_scope("return_terms"):
        entering = lax.all_to_all(entering, "tm", 0, 0)
    return pl.pallas_call(
        final_kernel,
        out_shape=shape(GROUPS, STEPS, lines, line_len),
        in_specs=[VMEM] * 7 + [HBM] + [VMEM] * 5,
        out_specs=HBM,
        scratch_shapes=[
            pltpu.VMEM((GROUPS, STEPS, lines, line_len), f32),
            held,
            pltpu.SemaphoreType.DMA((STEPS,)),
            pltpu.SemaphoreType.DMA,
        ],
        compiler_params=grant(20),
        name="final",
    )(entering.reshape(sections, LB), shift, weights, *own[:-1], in_hbm(own[-1]), *edges)


def solution(mesh):
    in_specs = (
        P("tm", None, "space", None),
        P("tm", "space", None),
        P("space"),
        P("space", None),
        P(),
        P(),
    )
    out_specs = P("tm", None, "space", None)
    return jax.shard_map(shards, mesh=mesh, in_specs=in_specs, out_specs=out_specs, check_vma=False)
```

```python
import functools

import jax
import jax.numpy as jnp
from jax import lax
from jax.experimental import pallas as pl
from jax.experimental.pallas import tpu as pltpu
from jax.sharding import PartitionSpec as P

LB = 128
GROUPS = 2
STEPS = 4
SLAB = 16
EDGE = 8
REACH = (11, 10, 9, 8, 7)
GROUP_ROWS = sum(REACH)
MESSAGE_ROWS = 96
VMEM = pl.BlockSpec(memory_space=pltpu.VMEM)
SMEM = pl.BlockSpec(memory_space=pltpu.SMEM)
HBM = pl.BlockSpec(memory_space=pltpu.HBM)
MEBI = 1024 * 1024


def columns(row):
    return jnp.broadcast_to(row, (LB, LB)).T


def class_masks(categories):
    even, odd, upper = [], [], []
    for category in categories:
        high = category > 1.5
        low = category - jnp.where(high, 2.0, 0.0)
        odd.append(jnp.where(low > 0.5, 1.0, 0.0).astype(jnp.bfloat16))
        even.append(jnp.where(low > 0.5, 0.0, 1.0).astype(jnp.bfloat16))
        upper.append(high)
    return even, odd, upper


def rates_of(categories, rates_ref):
    blocks = []
    for category in categories:
        rate = jnp.broadcast_to(rates_ref[0:1, :], category.shape)
        for c in range(1, 4):
            rate = jnp.where(category > c - 0.5, jnp.broadcast_to(rates_ref[c : c + 1, :], category.shape), rate)
        blocks.append(rate)
    return jnp.concatenate(blocks, axis=1)


def solve_field(field, masks, weights):
    even, odd, upper = masks
    rows = field.shape[0]
    left = []
    for block in range(2):
        x = field[:, block * LB : (block + 1) * LB]
        high = x.astype(jnp.bfloat16)
        low = (x - high.astype(jnp.float32)).astype(jnp.bfloat16)
        high_pair = [high * even[block], high * odd[block]]
        low_pair = [low * even[block], low * odd[block]]
        left.append(jnp.concatenate(high_pair + low_pair + high_pair, axis=1))
    weights = jnp.concatenate([weights[: 2 * LB], weights], axis=0)
    product = jnp.dot(jnp.concatenate(left, axis=0), weights, preferred_element_type=jnp.float32)
    blocks = []
    for block in range(2):
        part = product[block * rows : (block + 1) * rows]
        blocks.append(jnp.where(upper[block], part[:, LB:], part[:, :LB]))
    return jnp.concatenate(blocks, axis=1)


def solve_lines(fields, masks, weights):
    return [solve_field(field, masks, weights) for field in fields]


def spread(field, coupling):
    rows = field.shape[0]
    return field + coupling * (pltpu.roll(field, 1, 0) + pltpu.roll(field, rows - 1, 0))


def relaxations(starts, sources, coupling, categories, weights, rates_ref, first, relaxed_to):
    masks = class_masks(categories)
    linear, state = starts[0], starts
    for m in range(STEPS):
        *state, linear = solve_lines(
            [spread(state[g], coupling) + sources(g, m) for g in range(GROUPS)] + [spread(linear, coupling)],
            masks,
            weights,
        )
        if m < STEPS - 1:
            for g in range(GROUPS):
                relaxed_to(g, m, state[g])
    ends = state
    linear = jnp.where(first > 0, jnp.zeros_like(linear), linear)
    change = ends[0] - starts[1]
    resid, onward = change, ends[1]
    for m in range(STEPS):
        resid, onward = solve_lines([spread(resid, coupling), spread(onward, coupling)], masks, weights)
    rates = rates_of(categories, rates_ref)
    decay = jnp.exp(-rates)
    ahead = onward * jnp.exp(rates)
    held = decay * linear
    return dict(
        term=resid + ahead - held,
        shift=ends[1] - ahead,
        decay=decay,
        bases=(jnp.where(first > 0, jnp.zeros_like(linear), starts[0]), change - linear),
        last=ends[1] + resid - held,
    )


def pack_kernel(
    starts_hbm, sources_hbm, coupling_hbm, classes_hbm, rates_hbm,
    up_ref, down_ref, params_ref, starts_ref, sources_ref, rates_ref,
    starts_low, starts_high, sources_low, sources_high, coupling_row, classes_rows, sems,
):
    lines = starts_hbm.shape[1]
    low, high = pl.ds(0, SLAB), pl.ds(lines - SLAB, SLAB)
    pairs = [
        (sources_hbm.at[:, :, high, :], sources_high),
        (sources_hbm.at[:, :, low, :], sources_low),
        (starts_hbm.at[:, high, :], starts_high),
        (starts_hbm.at[:, low, :], starts_low),
        (coupling_hbm, coupling_row),
        (classes_hbm, classes_rows),
        (starts_hbm, starts_ref),
        (sources_hbm, sources_ref),
        (rates_hbm, rates_ref),
    ]
    whole = 3
    copies = [pltpu.make_async_copy(src, dst, sems.at[i]) for i, (src, dst) in enumerate(pairs)]
    for copy in copies:
        copy.start()
    for ref in (up_ref, down_ref, params_ref):
        ref[...] = jnp.zeros_like(ref)
    for copy in copies[:-whole]:
        copy.wait()
    params_ref[0:1, :] = coupling_row[...]
    params_ref[1:3, :] = classes_rows[...].astype(jnp.float32)
    for g in range(GROUPS):
        at = g * GROUP_ROWS
        for index, reach in enumerate(REACH):
            if index == 0:
                up, down = starts_high[g, SLAB - reach :, :], starts_low[g, :reach, :]
            else:
                up, down = sources_high[g, index - 1, SLAB - reach :, :], sources_low[g, index - 1, :reach, :]
            up_ref[at : at + reach, :] = up
            down_ref[at : at + reach, :] = down
            at += reach
    for ref in (up_ref, down_ref):
        ref[GROUPS * GROUP_ROWS : GROUPS * GROUP_ROWS + 3, :LB] = params_ref[0:3, :]
    for copy in copies[-whole:]:
        copy.wait()


def own_kernel(
    first_ref, starts_ref, sources_ref, params_ref, weights_ref, rates_ref,
    term_ref, shift_ref, decay_ref, base_ref, last_ref, relaxed_ref,
):
    coupling, *categories = [columns(params_ref[row : row + 1, :]) for row in range(3)]
    coupling = jnp.concatenate([coupling, coupling], axis=1)

    def relaxed_to(g, m, field):
        relaxed_ref[g, m] = field

    out = relaxations(
        [starts_ref[g] for g in range(GROUPS)], lambda g, m: sources_ref[g, m], coupling, categories, weights_ref[...],
        rates_ref, first_ref[0, 0], relaxed_to,
    )
    term_ref[...] = out["term"]
    shift_ref[...] = out["shift"]
    decay_ref[...] = out["decay"]
    base_ref[...] = out["bases"][1]
    last_ref[...] = out["last"]


def ends_of(strip, beyond):
    return jnp.concatenate([strip[16 - beyond : 24], strip[40 : 48 + beyond]], axis=0)


def joined(inner, ends):
    lines, half = inner.shape[0], ends.shape[0] // 2
    return jnp.concatenate([ends[:half], inner[EDGE : lines - EDGE], ends[half:]], axis=0)


def edge_kernel(
    first_ref, starts_ref, sources_ref, params_ref, above_ref, below_ref, weights_ref, rates_ref,
    own_term_ref, own_shift_ref, own_decay_ref,
    terms_ref, factors_ref, shift_ref, decay_ref, base_ref, last_ref, relaxed_ref, halo_ref,
):
    lines = starts_ref.shape[1]
    lane = lax.broadcasted_iota(jnp.int32, (8, LB), 1)
    at = GROUPS * GROUP_ROWS
    own = params_ref[...]
    halo_ref[...] = jnp.zeros_like(halo_ref)
    halo_ref[0, 0:3, :LB] = above_ref[at : at + 3, :LB]
    halo_ref[0, 8:11, :LB] = below_ref[at : at + 3, :LB]
    above, below = halo_ref[0, 0:8, :LB], halo_ref[0, 8:16, :LB]
    upper = jnp.where(lane < SLAB, pltpu.roll(above, SLAB, 1), pltpu.roll(own, SLAB, 1))
    lower = jnp.where(lane < 3 * SLAB, pltpu.roll(own, 3 * SLAB, 1), pltpu.roll(below, 3 * SLAB, 1))
    strip = jnp.where(lane < 2 * SLAB, upper, lower)
    rows = 4 * SLAB
    coupling, *categories = [columns(strip[row : row + 1])[:rows] for row in range(3)]
    coupling = jnp.concatenate([coupling, coupling], axis=1)

    halo_ref[0, 0:16, :] = jnp.zeros((16, 2 * LB), jnp.float32)
    for g in range(GROUPS):
        at = g * GROUP_ROWS
        for index, reach in enumerate(REACH):
            slab = g * len(REACH) + index
            halo_ref[slab, SLAB - reach : SLAB, :] = above_ref[at : at + reach, :]
            halo_ref[slab, SLAB : SLAB + reach, :] = below_ref[at : at + reach, :]
            at += reach

    def strips(slab, low, high):
        return jnp.concatenate([halo_ref[slab, :SLAB, :], low, high, halo_ref[slab, SLAB:, :]], axis=0)

    starts = [
        strips(g * len(REACH), starts_ref[g, :SLAB, :], starts_ref[g, lines - SLAB :, :]) for g in range(GROUPS)
    ]

    def sources(g, m):
        return strips(
            g * len(REACH) + 1 + m, sources_ref[g, m, :SLAB, :], sources_ref[g, m, lines - SLAB :, :]
        )

    def relaxed_to(g, m, field):
        relaxed_ref[g, m] = ends_of(field, 0)

    out = relaxations(starts, sources, coupling, categories, weights_ref[...], rates_ref, first_ref[0, 0], relaxed_to)
    section = lines + 2 * EDGE
    end_decay = ends_of(out["decay"], EDGE)
    decay = joined(own_decay_ref[...], end_decay)
    term = joined(own_term_ref[...], ends_of(out["term"], EDGE))
    for block in range(2):
        at = block * section
        lanes = slice(block * LB, (block + 1) * LB)
        terms_ref[at : at + section, :] = term[:, lanes]
        factors_ref[at : at + section, :] = (decay * decay)[:, lanes]
    shift_ref[...] = joined(own_shift_ref[...], ends_of(out["shift"], EDGE))
    decay_ref[...] = end_decay
    for g in range(GROUPS):
        base_ref[g] = ends_of(out["bases"][g], EDGE)
    last_ref[...] = ends_of(out["last"], 0)


def scan_kernel(place_ref, terms_ref, factors_ref, entering_ref):
    factor = factors_ref[place_ref[0, 0]]
    carried = jnp.zeros_like(factor)
    for d in range(terms_ref.shape[0]):
        entering_ref[d] = carried
        carried = factor * carried + terms_ref[d]


def final_kernel(
    first_ref, entering_ref, shift_ref, params_ref, above_ref, below_ref, weights_ref, starts_ref,
    decay_ref, base_ref, last_ref, relaxed_ref, edge_decay_ref, edge_base_ref, edge_last_ref, edge_relaxed_ref, states_hbm, states_ref, sems,
):
    lines = last_ref.shape[0]
    section = lines + 2 * EDGE
    at = GROUPS * GROUP_ROWS

    def along(row):
        own = columns(params_ref[row : row + 1, :])
        above = columns(above_ref[at + row : at + row + 1, :LB])
        below = columns(below_ref[at + row : at + row + 1, :LB])
        return jnp.concatenate([above[lines - EDGE :], own, below[:EDGE]], axis=0)

    coupling, *categories = [along(row) for row in range(3)]
    coupling = jnp.concatenate([coupling, coupling], axis=1)
    masks = class_masks(categories)

    entering = jnp.concatenate([entering_ref[:section, :], entering_ref[section:, :]], axis=1)
    shift = shift_ref[...]
    inner = slice(EDGE, EDGE + lines)
    decay = joined(decay_ref[...], edge_decay_ref[...])
    start = jnp.where(first_ref[0, 0] > 0, 0.0, 1.0) * starts_ref[0]
    base = [joined(start, edge_base_ref[0]), joined(base_ref[...], edge_base_ref[1])]
    last = [base[1][inner] + starts_ref[1], joined(last_ref[...], edge_last_ref[...])]
    passed = decay * entering

    def send(m):
        copy = pltpu.make_async_copy(states_ref.at[:, m], states_hbm.at[:, m], sems.at[m])
        copy.start()
        return copy

    states_ref[0, 3] = passed[inner] + last[0]
    states_ref[1, 3] = (decay * passed)[inner] + last[1]
    copies = [send(3)]
    state = [entering + shift - base[0], passed + base[1]]
    weights = weights_ref[...]
    for m in range(STEPS - 1):
        state = solve_lines([spread(s, coupling) for s in state], masks, weights)
        for g in range(GROUPS):
            states_ref[g, m] = joined(relaxed_ref[g, m], edge_relaxed_ref[g, m]) + state[g][inner]
        copies.append(send(m))
    for copy in copies:
        copy.wait()


def shards(sources, starts, coupling, classes, inverses, coarse_rate):
    count, along = lax.axis_size("tm"), lax.axis_size("space")
    lines, line_len = starts.shape[1:]
    near_rows = lines + 2 * EDGE
    sections = 2 * near_rows
    f32 = jnp.float32
    place = lax.axis_index("tm").astype(jnp.int32).reshape(1, 1)
    first = (lax.axis_index("tm") == 0).astype(jnp.int32).reshape(1, 1)

    def grant(size):
        return pltpu.CompilerParams(vmem_limit_bytes=size * MEBI)

    def shape(*dims):
        return jax.ShapeDtypeStruct(dims, f32)

    message = shape(MESSAGE_ROWS, line_len)
    up, down, params, held_starts, held_sources, rates = pl.pallas_call(
        pack_kernel,
        out_shape=(message, message, shape(8, lines), *[shape(*x.shape) for x in (starts, sources, coarse_rate)]),
        in_specs=[HBM] * 5,
        out_specs=[VMEM] * 6,
        scratch_shapes=[
            pltpu.VMEM((GROUPS, SLAB, line_len), f32),
            pltpu.VMEM((GROUPS, SLAB, line_len), f32),
            pltpu.VMEM((GROUPS, STEPS, SLAB, line_len), f32),
            pltpu.VMEM((GROUPS, STEPS, SLAB, line_len), f32),
            pltpu.VMEM((1, lines), f32),
            pltpu.VMEM((2, lines), jnp.int32),
            pltpu.SemaphoreType.DMA((9,)),
        ],
        compiler_params=grant(6),
        name="pack",
    )(*[
        pltpu.with_memory_space_constraint(x, pltpu.HBM)
        for x in (starts, sources, coupling.reshape(1, lines), classes.T, coarse_rate)
    ])

    with jax.named_scope("halo"):
        upward = [(i, i + 1) for i in range(along - 1)]
        above = lax.ppermute(up, "space", upward)
        below = lax.ppermute(down, "space", [(j, i) for i, j in upward])

    with jax.named_scope("weights"):
        transposed = inverses.transpose(0, 2, 1)
        table = jnp.concatenate(
            [
                jnp.concatenate([transposed[0], transposed[2]], axis=1),
                jnp.concatenate([transposed[1], transposed[3]], axis=1),
            ],
            axis=0,
        )
        high = lax.reduce_precision(table, 8, 7)
        weights = jnp.concatenate([high, table - high], axis=0).astype(jnp.bfloat16)

    def relaxed(rows):
        return shape(GROUPS, STEPS - 1, rows, line_len)

    term, shift, *own = pl.pallas_call(
        own_kernel,
        out_shape=(*[shape(lines, line_len)] * 5, relaxed(lines)),
        in_specs=[SMEM] + [VMEM] * 5,
        out_specs=[VMEM] * 6,
        compiler_params=grant(24),
        cost_estimate=pl.CostEstimate(flops=5_000_000_000, bytes_accessed=4_000_000, transcendentals=0),
        name="own",
    )(first, held_starts, held_sources, params, weights, rates)
    terms, factors, shift, *edges = pl.pallas_call(
        edge_kernel,
        out_shape=(
            shape(sections, LB),
            shape(sections, LB),
            shape(near_rows, line_len),
            shape(4 * EDGE, line_len),
            shape(GROUPS, 4 * EDGE, line_len),
            shape(2 * EDGE, line_len),
            relaxed(2 * EDGE),
        ),
        in_specs=[SMEM] + [VMEM] * 10,
        out_specs=[VMEM] * 7,
        scratch_shapes=[pltpu.VMEM((GROUPS * len(REACH), 2 * SLAB, line_len), f32)],
        compiler_params=grant(20),
        name="edge",
    )(first, held_starts, held_sources, params, above, below, weights, rates, term, shift, own[0])

    split = (count, 1, sections * LB // count)
    with jax.named_scope("onward"):
        shift = lax.ppermute(shift, "tm", [(i, i + 1) for i in range(count - 1)])
    with jax.named_scope("gather_terms"):
        terms = lax.all_to_all(terms.reshape(split), "tm", 0, 0)
    entering = pl.pallas_call(
        scan_kernel,
        out_shape=shape(*split),
        in_specs=[SMEM] + [VMEM] * 2,
        out_specs=VMEM,
        compiler_params=grant(4),
        name="scan",
    )(place, terms, factors.reshape(split))
    with jax.named_scope("return_terms"):
        entering = lax.all_to_all(entering, "tm", 0, 0)
    return pl.pallas_call(
        final_kernel,
        out_shape=shape(GROUPS, STEPS, lines, line_len),
        in_specs=[SMEM] + [VMEM] * 15,
        out_specs=HBM,
        scratch_shapes=[
            pltpu.VMEM((GROUPS, STEPS, lines, line_len), f32),
            pltpu.SemaphoreType.DMA((STEPS,)),
        ],
        compiler_params=grant(20),
        name="final",
    )(first, entering.reshape(sections, LB), shift, params, above, below, weights, held_starts, *own, *edges)


def solution(mesh):
    in_specs = (
        P("tm", None, "space", None),
        P("tm", "space", None),
        P("space"),
        P("space", None),
        P(),
        P(),
    )
    out_specs = P("tm", None, "space", None)
    return jax.shard_map(shards, mesh=mesh, in_specs=in_specs, out_specs=out_specs, check_vma=False)
```

```python
import functools

import jax
import jax.numpy as jnp
from jax import lax
from jax.experimental import pallas as pl
from jax.experimental.pallas import tpu as pltpu
from jax.sharding import PartitionSpec as P

LB = 128
GROUPS = 2
STEPS = 4
SLAB = 16
EDGE = 8
REACH = (11, 10, 9, 8, 7)
GROUP_ROWS = sum(REACH)
MESSAGE_ROWS = 96
VMEM = pl.BlockSpec(memory_space=pltpu.VMEM)
SMEM = pl.BlockSpec(memory_space=pltpu.SMEM)
HBM = pl.BlockSpec(memory_space=pltpu.HBM)
MEBI = 1024 * 1024


def columns(row):
    return jnp.broadcast_to(row, (LB, LB)).T


def class_masks(categories):
    even, odd, upper = [], [], []
    for category in categories:
        high = category > 1.5
        low = category - jnp.where(high, 2.0, 0.0)
        odd.append(jnp.where(low > 0.5, 1.0, 0.0).astype(jnp.bfloat16))
        even.append(jnp.where(low > 0.5, 0.0, 1.0).astype(jnp.bfloat16))
        upper.append(high)
    return even, odd, upper


def rates_of(categories, rates_ref):
    blocks = []
    for category in categories:
        rate = jnp.broadcast_to(rates_ref[0:1, :], category.shape)
        for c in range(1, 4):
            rate = jnp.where(category > c - 0.5, jnp.broadcast_to(rates_ref[c : c + 1, :], category.shape), rate)
        blocks.append(rate)
    return jnp.concatenate(blocks, axis=1)


def solve_field(field, masks, weights):
    even, odd, upper = masks
    rows = field.shape[0]
    left = []
    for block in range(2):
        x = field[:, block * LB : (block + 1) * LB]
        high = x.astype(jnp.bfloat16)
        low = (x - high.astype(jnp.float32)).astype(jnp.bfloat16)
        high_pair = [high * even[block], high * odd[block]]
        low_pair = [low * even[block], low * odd[block]]
        left.append(jnp.concatenate(high_pair + low_pair + high_pair, axis=1))
    weights = jnp.concatenate([weights[: 2 * LB], weights], axis=0)
    product = jnp.dot(jnp.concatenate(left, axis=0), weights, preferred_element_type=jnp.float32)
    blocks = []
    for block in range(2):
        part = product[block * rows : (block + 1) * rows]
        blocks.append(jnp.where(upper[block], part[:, LB:], part[:, :LB]))
    return jnp.concatenate(blocks, axis=1)


def solve_lines(fields, masks, weights):
    return [solve_field(field, masks, weights) for field in fields]


def spread(field, coupling):
    rows = field.shape[0]
    return field + coupling * (pltpu.roll(field, 1, 0) + pltpu.roll(field, rows - 1, 0))


def relaxations(starts, sources, coupling, categories, weights, rates_ref, first, relaxed_to):
    masks = class_masks(categories)
    linear, state = starts[0], starts
    for m in range(STEPS):
        *state, linear = solve_lines(
            [spread(state[g], coupling) + sources(g, m) for g in range(GROUPS)] + [spread(linear, coupling)],
            masks,
            weights,
        )
        if m < STEPS - 1:
            for g in range(GROUPS):
                relaxed_to(g, m, state[g])
    ends = state
    linear = jnp.where(first > 0, jnp.zeros_like(linear), linear)
    change = ends[0] - starts[1]
    resid, onward = change, ends[1]
    for m in range(STEPS):
        resid, onward = solve_lines([spread(resid, coupling), spread(onward, coupling)], masks, weights)
    rates = rates_of(categories, rates_ref)
    decay = jnp.exp(-rates)
    ahead = onward * jnp.exp(rates)
    held = decay * linear
    return dict(
        term=resid + ahead - held,
        shift=ends[1] - ahead,
        decay=decay,
        bases=(jnp.where(first > 0, jnp.zeros_like(linear), starts[0]), change - linear),
        last=ends[1] + resid - held,
    )


def pack_kernel(
    starts_hbm, sources_hbm, coupling_hbm, classes_hbm, rates_hbm, inverses_hbm,
    up_ref, down_ref, params_ref, starts_ref, sources_ref, rates_ref, weights_ref,
    starts_low, starts_high, sources_low, sources_high, coupling_row, classes_rows, inverses_ref, sems,
):
    lines = starts_hbm.shape[1]
    low, high = pl.ds(0, SLAB), pl.ds(lines - SLAB, SLAB)
    pairs = [
        (sources_hbm.at[:, :, high, :], sources_high),
        (sources_hbm.at[:, :, low, :], sources_low),
        (starts_hbm.at[:, high, :], starts_high),
        (starts_hbm.at[:, low, :], starts_low),
        (coupling_hbm, coupling_row),
        (classes_hbm, classes_rows),
        (inverses_hbm, inverses_ref),
        (starts_hbm, starts_ref),
        (sources_hbm, sources_ref),
        (rates_hbm, rates_ref),
    ]
    whole = 3
    copies = [pltpu.make_async_copy(src, dst, sems.at[i]) for i, (src, dst) in enumerate(pairs)]
    for copy in copies:
        copy.start()
    for ref in (up_ref, down_ref, params_ref):
        ref[...] = jnp.zeros_like(ref)
    for copy in copies[:-whole]:
        copy.wait()
    params_ref[0:1, :] = coupling_row[...]
    params_ref[1:3, :] = classes_rows[...].astype(jnp.float32)
    for g in range(GROUPS):
        at = g * GROUP_ROWS
        for index, reach in enumerate(REACH):
            if index == 0:
                up, down = starts_high[g, SLAB - reach :, :], starts_low[g, :reach, :]
            else:
                up, down = sources_high[g, index - 1, SLAB - reach :, :], sources_low[g, index - 1, :reach, :]
            up_ref[at : at + reach, :] = up
            down_ref[at : at + reach, :] = down
            at += reach
    for ref in (up_ref, down_ref):
        ref[GROUPS * GROUP_ROWS : GROUPS * GROUP_ROWS + 3, :LB] = params_ref[0:3, :]
    for c in range(4):
        transposed = inverses_ref[c].T
        rounded = transposed.astype(jnp.bfloat16)
        rest = (transposed - rounded.astype(jnp.float32)).astype(jnp.bfloat16)
        row, lane = c % 2 * LB, c // 2 * LB
        weights_ref[row : row + LB, lane : lane + LB] = rounded
        weights_ref[2 * LB + row : 3 * LB + row, lane : lane + LB] = rest
    for copy in copies[-whole:]:
        copy.wait()


def own_kernel(
    first_ref, starts_ref, sources_ref, params_ref, weights_ref, rates_ref,
    term_ref, shift_ref, decay_ref, base_ref, last_ref, relaxed_ref,
):
    coupling, *categories = [columns(params_ref[row : row + 1, :]) for row in range(3)]
    coupling = jnp.concatenate([coupling, coupling], axis=1)

    def relaxed_to(g, m, field):
        relaxed_ref[g, m] = field

    out = relaxations(
        [starts_ref[g] for g in range(GROUPS)], lambda g, m: sources_ref[g, m], coupling, categories, weights_ref[...],
        rates_ref, first_ref[0, 0], relaxed_to,
    )
    term_ref[...] = out["term"]
    shift_ref[...] = out["shift"]
    decay_ref[...] = out["decay"]
    base_ref[...] = out["bases"][1]
    last_ref[...] = out["last"]


def ends_of(strip, beyond):
    return jnp.concatenate([strip[16 - beyond : 24], strip[40 : 48 + beyond]], axis=0)


def joined(inner, ends):
    lines, half = inner.shape[0], ends.shape[0] // 2
    return jnp.concatenate([ends[:half], inner[EDGE : lines - EDGE], ends[half:]], axis=0)


def edge_kernel(
    first_ref, starts_ref, sources_ref, params_ref, above_ref, below_ref, weights_ref, rates_ref,
    own_term_ref, own_shift_ref, own_decay_ref,
    terms_ref, factors_ref, shift_ref, decay_ref, base_ref, last_ref, relaxed_ref, halo_ref,
):
    lines = starts_ref.shape[1]
    lane = lax.broadcasted_iota(jnp.int32, (8, LB), 1)
    at = GROUPS * GROUP_ROWS
    own = params_ref[...]
    halo_ref[...] = jnp.zeros_like(halo_ref)
    halo_ref[0, 0:3, :LB] = above_ref[at : at + 3, :LB]
    halo_ref[0, 8:11, :LB] = below_ref[at : at + 3, :LB]
    above, below = halo_ref[0, 0:8, :LB], halo_ref[0, 8:16, :LB]
    upper = jnp.where(lane < SLAB, pltpu.roll(above, SLAB, 1), pltpu.roll(own, SLAB, 1))
    lower = jnp.where(lane < 3 * SLAB, pltpu.roll(own, 3 * SLAB, 1), pltpu.roll(below, 3 * SLAB, 1))
    strip = jnp.where(lane < 2 * SLAB, upper, lower)
    rows = 4 * SLAB
    coupling, *categories = [columns(strip[row : row + 1])[:rows] for row in range(3)]
    coupling = jnp.concatenate([coupling, coupling], axis=1)

    halo_ref[0, 0:16, :] = jnp.zeros((16, 2 * LB), jnp.float32)
    for g in range(GROUPS):
        at = g * GROUP_ROWS
        for index, reach in enumerate(REACH):
            slab = g * len(REACH) + index
            halo_ref[slab, SLAB - reach : SLAB, :] = above_ref[at : at + reach, :]
            halo_ref[slab, SLAB : SLAB + reach, :] = below_ref[at : at + reach, :]
            at += reach

    def strips(slab, low, high):
        return jnp.concatenate([halo_ref[slab, :SLAB, :], low, high, halo_ref[slab, SLAB:, :]], axis=0)

    starts = [
        strips(g * len(REACH), starts_ref[g, :SLAB, :], starts_ref[g, lines - SLAB :, :]) for g in range(GROUPS)
    ]

    def sources(g, m):
        return strips(
            g * len(REACH) + 1 + m, sources_ref[g, m, :SLAB, :], sources_ref[g, m, lines - SLAB :, :]
        )

    def relaxed_to(g, m, field):
        relaxed_ref[g, m] = ends_of(field, 0)

    out = relaxations(starts, sources, coupling, categories, weights_ref[...], rates_ref, first_ref[0, 0], relaxed_to)
    section = lines + 2 * EDGE
    end_decay = ends_of(out["decay"], EDGE)
    decay = joined(own_decay_ref[...], end_decay)
    term = joined(own_term_ref[...], ends_of(out["term"], EDGE))
    for block in range(2):
        at = block * section
        lanes = slice(block * LB, (block + 1) * LB)
        terms_ref[at : at + section, :] = term[:, lanes]
        factors_ref[at : at + section, :] = (decay * decay)[:, lanes]
    shift_ref[...] = joined(own_shift_ref[...], ends_of(out["shift"], EDGE))
    decay_ref[...] = end_decay
    for g in range(GROUPS):
        base_ref[g] = ends_of(out["bases"][g], EDGE)
    last_ref[...] = ends_of(out["last"], 0)


def scan_kernel(place_ref, terms_ref, factors_ref, entering_ref):
    factor = factors_ref[place_ref[0, 0]]
    carried = jnp.zeros_like(factor)
    for d in range(terms_ref.shape[0]):
        entering_ref[d] = carried
        carried = factor * carried + terms_ref[d]


def lines_kernel(params_ref, above_ref, below_ref, coupling_ref, masks_ref, upper_ref):
    lines = params_ref.shape[1]
    at = GROUPS * GROUP_ROWS

    def along(row):
        own = columns(params_ref[row : row + 1, :])
        above = columns(above_ref[at + row : at + row + 1, :LB])
        below = columns(below_ref[at + row : at + row + 1, :LB])
        return jnp.concatenate([above[lines - EDGE :], own, below[:EDGE]], axis=0)

    coupling_ref[...] = along(0)
    even, odd, upper = class_masks([along(1), along(2)])
    for block in range(2):
        masks_ref[0, block] = even[block]
        masks_ref[1, block] = odd[block]
        upper_ref[block] = jnp.where(upper[block], 1.0, 0.0)


def final_kernel(
    first_ref, entering_ref, shift_ref, coupling_ref, masks_ref, upper_ref, weights_ref, starts_ref,
    decay_ref, base_ref, last_ref, relaxed_ref, edge_decay_ref, edge_base_ref, edge_last_ref, edge_relaxed_ref, states_hbm, states_ref, sems,
):
    lines = last_ref.shape[0]
    section = lines + 2 * EDGE
    coupling = jnp.concatenate([coupling_ref[...], coupling_ref[...]], axis=1)
    masks = (
        [masks_ref[0, block] for block in range(2)],
        [masks_ref[1, block] for block in range(2)],
        [upper_ref[block] > 0.5 for block in range(2)],
    )

    entering = jnp.concatenate([entering_ref[:section, :], entering_ref[section:, :]], axis=1)
    shift = shift_ref[...]
    inner = slice(EDGE, EDGE + lines)
    decay = joined(decay_ref[...], edge_decay_ref[...])
    start = jnp.where(first_ref[0, 0] > 0, 0.0, 1.0) * starts_ref[0]
    base = [joined(start, edge_base_ref[0]), joined(base_ref[...], edge_base_ref[1])]
    last = [base[1][inner] + starts_ref[1], joined(last_ref[...], edge_last_ref[...])]
    passed = decay * entering

    def send(m):
        copy = pltpu.make_async_copy(states_ref.at[:, m], states_hbm.at[:, m], sems.at[m])
        copy.start()
        return copy

    states_ref[0, 3] = passed[inner] + last[0]
    states_ref[1, 3] = (decay * passed)[inner] + last[1]
    copies = [send(3)]
    state = [entering + shift - base[0], passed + base[1]]
    weights = weights_ref[...]
    for m in range(STEPS - 1):
        state = solve_lines([spread(s, coupling) for s in state], masks, weights)
        for g in range(GROUPS):
            states_ref[g, m] = joined(relaxed_ref[g, m], edge_relaxed_ref[g, m]) + state[g][inner]
        copies.append(send(m))
    for copy in copies:
        copy.wait()


def shards(sources, starts, coupling, classes, inverses, coarse_rate):
    count, along = lax.axis_size("tm"), lax.axis_size("space")
    lines, line_len = starts.shape[1:]
    near_rows = lines + 2 * EDGE
    sections = 2 * near_rows
    f32 = jnp.float32
    place = lax.axis_index("tm").astype(jnp.int32).reshape(1, 1)
    first = (lax.axis_index("tm") == 0).astype(jnp.int32).reshape(1, 1)

    def grant(size):
        return pltpu.CompilerParams(vmem_limit_bytes=size * MEBI)

    def shape(*dims):
        return jax.ShapeDtypeStruct(dims, f32)

    message = shape(MESSAGE_ROWS, line_len)
    up, down, params, held_starts, held_sources, rates, weights = pl.pallas_call(
        pack_kernel,
        out_shape=(
            message,
            message,
            shape(8, lines),
            *[shape(*x.shape) for x in (starts, sources, coarse_rate)],
            jax.ShapeDtypeStruct((4 * LB, 2 * LB), jnp.bfloat16),
        ),
        in_specs=[HBM] * 6,
        out_specs=[VMEM] * 7,
        scratch_shapes=[
            pltpu.VMEM((GROUPS, SLAB, line_len), f32),
            pltpu.VMEM((GROUPS, SLAB, line_len), f32),
            pltpu.VMEM((GROUPS, STEPS, SLAB, line_len), f32),
            pltpu.VMEM((GROUPS, STEPS, SLAB, line_len), f32),
            pltpu.VMEM((1, lines), f32),
            pltpu.VMEM((2, lines), jnp.int32),
            pltpu.VMEM(inverses.shape, f32),
            pltpu.SemaphoreType.DMA((10,)),
        ],
        compiler_params=grant(6),
        name="pack",
    )(*[
        pltpu.with_memory_space_constraint(x, pltpu.HBM)
        for x in (starts, sources, coupling.reshape(1, lines), classes.T, coarse_rate, inverses)
    ])

    with jax.named_scope("halo"):
        upward = [(i, i + 1) for i in range(along - 1)]
        above = lax.ppermute(up, "space", upward)
        below = lax.ppermute(down, "space", [(j, i) for i, j in upward])

    def relaxed(rows):
        return shape(GROUPS, STEPS - 1, rows, line_len)

    term, shift, *own = pl.pallas_call(
        own_kernel,
        out_shape=(*[shape(lines, line_len)] * 5, relaxed(lines)),
        in_specs=[SMEM] + [VMEM] * 5,
        out_specs=[VMEM] * 6,
        compiler_params=grant(24),
        cost_estimate=pl.CostEstimate(flops=5_000_000_000, bytes_accessed=4_000_000, transcendentals=0),
        name="own",
    )(first, held_starts, held_sources, params, weights, rates)
    terms, factors, shift, *edges = pl.pallas_call(
        edge_kernel,
        out_shape=(
            shape(sections, LB),
            shape(sections, LB),
            shape(near_rows, line_len),
            shape(4 * EDGE, line_len),
            shape(GROUPS, 4 * EDGE, line_len),
            shape(2 * EDGE, line_len),
            relaxed(2 * EDGE),
        ),
        in_specs=[SMEM] + [VMEM] * 10,
        out_specs=[VMEM] * 7,
        scratch_shapes=[pltpu.VMEM((GROUPS * len(REACH), 2 * SLAB, line_len), f32)],
        compiler_params=grant(20),
        name="edge",
    )(first, held_starts, held_sources, params, above, below, weights, rates, term, shift, own[0])

    split = (count, 1, sections * LB // count)
    with jax.named_scope("onward"):
        shift = lax.ppermute(shift, "tm", [(i, i + 1) for i in range(count - 1)])
    with jax.named_scope("gather_terms"):
        terms = lax.all_to_all(terms.reshape(split), "tm", 0, 0)
    entering = pl.pallas_call(
        scan_kernel,
        out_shape=shape(*split),
        in_specs=[SMEM] + [VMEM] * 2,
        out_specs=VMEM,
        compiler_params=grant(4),
        name="scan",
    )(place, terms, factors.reshape(split))
    with jax.named_scope("return_terms"):
        entering = lax.all_to_all(entering, "tm", 0, 0)
    spread_lines = pl.pallas_call(
        lines_kernel,
        out_shape=(
            shape(near_rows, LB),
            jax.ShapeDtypeStruct((2, 2, near_rows, LB), jnp.bfloat16),
            shape(2, near_rows, LB),
        ),
        in_specs=[VMEM] * 3,
        out_specs=[VMEM] * 3,
        compiler_params=grant(4),
        cost_estimate=pl.CostEstimate(flops=1_000_000_000, bytes_accessed=1_000_000, transcendentals=0),
        name="lines",
    )(params, above, below)
    return pl.pallas_call(
        final_kernel,
        out_shape=shape(GROUPS, STEPS, lines, line_len),
        in_specs=[SMEM] + [VMEM] * 15,
        out_specs=HBM,
        scratch_shapes=[
            pltpu.VMEM((GROUPS, STEPS, lines, line_len), f32),
            pltpu.SemaphoreType.DMA((STEPS,)),
        ],
        compiler_params=grant(20),
        name="final",
    )(first, entering.reshape(sections, LB), shift, *spread_lines, weights, held_starts, *own, *edges)


def solution(mesh):
    in_specs = (
        P("tm", None, "space", None),
        P("tm", "space", None),
        P("space"),
        P("space", None),
        P(),
        P(),
    )
    out_specs = P("tm", None, "space", None)
    return jax.shard_map(shards, mesh=mesh, in_specs=in_specs, out_specs=out_specs, check_vma=False)
```

```python
import functools

import jax
import jax.numpy as jnp
from jax import lax
from jax.experimental import pallas as pl
from jax.experimental.pallas import tpu as pltpu
from jax.sharding import PartitionSpec as P

LB = 128
GROUPS = 2
STEPS = 4
SLAB = 16
EDGE = 8
REACH = (11, 10, 9, 8, 7)
GROUP_ROWS = sum(REACH)
MESSAGE_ROWS = 96
VMEM = pl.BlockSpec(memory_space=pltpu.VMEM)
SMEM = pl.BlockSpec(memory_space=pltpu.SMEM)
HBM = pl.BlockSpec(memory_space=pltpu.HBM)
MEBI = 1024 * 1024


def columns(row):
    return jnp.broadcast_to(row, (LB, LB)).T


def class_masks(categories):
    even, odd, upper = [], [], []
    for category in categories:
        high = category > 1.5
        low = category - jnp.where(high, 2.0, 0.0)
        odd.append(jnp.where(low > 0.5, 1.0, 0.0).astype(jnp.bfloat16))
        even.append(jnp.where(low > 0.5, 0.0, 1.0).astype(jnp.bfloat16))
        upper.append(high)
    return even, odd, upper


def rates_of(categories, rates_ref):
    blocks = []
    for category in categories:
        rate = jnp.broadcast_to(rates_ref[0:1, :], category.shape)
        for c in range(1, 4):
            rate = jnp.where(category > c - 0.5, jnp.broadcast_to(rates_ref[c : c + 1, :], category.shape), rate)
        blocks.append(rate)
    return jnp.concatenate(blocks, axis=1)


def solve_field(field, masks, weights):
    even, odd, upper = masks
    rows = field.shape[0]
    highs, lows = [], []
    for block in range(2):
        x = field[:, block * LB : (block + 1) * LB]
        high = x.astype(jnp.bfloat16)
        low = (x - high.astype(jnp.float32)).astype(jnp.bfloat16)
        highs.append(jnp.concatenate([high * even[block], high * odd[block]], axis=1))
        lows.append(jnp.concatenate([low * even[block], low * odd[block]], axis=1))
    highs, lows = jnp.concatenate(highs, axis=0), jnp.concatenate(lows, axis=0)
    pairs = ((highs, weights[: 2 * LB]), (lows, weights[: 2 * LB]), (highs, weights[2 * LB :]))
    products = [jnp.dot(left, right, preferred_element_type=jnp.float32) for left, right in pairs]
    blocks = []
    for block in range(2):
        parts = [product[block * rows : (block + 1) * rows] for product in products]
        first, second, third = [jnp.where(upper[block], part[:, LB:], part[:, :LB]) for part in parts]
        blocks.append(first + second + third)
    return jnp.concatenate(blocks, axis=1)


def solve_lines(fields, masks, weights):
    return [solve_field(field, masks, weights) for field in fields]


def spread(field, coupling):
    rows = field.shape[0]
    return field + coupling * (pltpu.roll(field, 1, 0) + pltpu.roll(field, rows - 1, 0))


def relaxations(starts, sources, coupling, categories, weights, rates_ref, first, relaxed_to):
    masks = class_masks(categories)
    linear, state = starts[0], starts
    for m in range(STEPS):
        *state, linear = solve_lines(
            [spread(state[g], coupling) + sources(g, m) for g in range(GROUPS)] + [spread(linear, coupling)],
            masks,
            weights,
        )
        if m < STEPS - 1:
            for g in range(GROUPS):
                relaxed_to(g, m, state[g])
    ends = state
    linear = jnp.where(first > 0, jnp.zeros_like(linear), linear)
    change = ends[0] - starts[1]
    resid, onward = change, ends[1]
    for m in range(STEPS):
        resid, onward = solve_lines([spread(resid, coupling), spread(onward, coupling)], masks, weights)
    rates = rates_of(categories, rates_ref)
    decay = jnp.exp(-rates)
    ahead = onward * jnp.exp(rates)
    held = decay * linear
    return dict(
        term=resid + ahead - held,
        shift=ends[1] - ahead,
        decay=decay,
        bases=(jnp.where(first > 0, jnp.zeros_like(linear), starts[0]), change - linear),
        last=ends[1] + resid - held,
    )


def pack_kernel(
    starts_hbm, sources_hbm, coupling_hbm, classes_hbm, rates_hbm, inverses_hbm,
    up_ref, down_ref, params_ref, starts_ref, sources_ref, rates_ref, weights_ref,
    coupling_row, classes_rows, inverses_ref, sems,
):
    lines = starts_hbm.shape[1]
    pairs = [
        (inverses_hbm, inverses_ref),
        (coupling_hbm, coupling_row),
        (classes_hbm, classes_rows),
        *[(starts_hbm.at[g], starts_ref.at[g]) for g in range(GROUPS)],
        *[(sources_hbm.at[g, m], sources_ref.at[g, m]) for g in range(GROUPS) for m in range(STEPS)],
        (rates_hbm, rates_ref),
    ]
    copies = [pltpu.make_async_copy(src, dst, sems.at[i]) for i, (src, dst) in enumerate(pairs)]
    for copy in copies:
        copy.start()
    for ref in (up_ref, down_ref, params_ref):
        ref[...] = jnp.zeros_like(ref)
    for copy in copies[:3]:
        copy.wait()
    params_ref[0:1, :] = coupling_row[...]
    params_ref[1:3, :] = classes_rows[...].astype(jnp.float32)
    for c in range(4):
        transposed = inverses_ref[c].T
        rounded = transposed.astype(jnp.bfloat16)
        rest = (transposed - rounded.astype(jnp.float32)).astype(jnp.bfloat16)
        row, lane = c % 2 * LB, c // 2 * LB
        weights_ref[row : row + LB, lane : lane + LB] = rounded
        weights_ref[2 * LB + row : 3 * LB + row, lane : lane + LB] = rest
    for copy in copies[3:]:
        copy.wait()
    for g in range(GROUPS):
        at = g * GROUP_ROWS
        for index, reach in enumerate(REACH):
            if index == 0:
                own = starts_ref.at[g]
            else:
                own = sources_ref.at[g, index - 1]
            up_ref[at : at + reach, :] = own[lines - reach :, :]
            down_ref[at : at + reach, :] = own[:reach, :]
            at += reach
    for ref in (up_ref, down_ref):
        ref[GROUPS * GROUP_ROWS : GROUPS * GROUP_ROWS + 3, :LB] = params_ref[0:3, :]


def own_kernel(
    first_ref, starts_ref, sources_ref, params_ref, weights_ref, rates_ref,
    term_ref, shift_ref, decay_ref, base_ref, last_ref, relaxed_ref,
):
    coupling, *categories = [columns(params_ref[row : row + 1, :]) for row in range(3)]
    coupling = jnp.concatenate([coupling, coupling], axis=1)

    def relaxed_to(g, m, field):
        relaxed_ref[g, m] = field

    out = relaxations(
        [starts_ref[g] for g in range(GROUPS)], lambda g, m: sources_ref[g, m], coupling, categories, weights_ref[...],
        rates_ref, first_ref[0, 0], relaxed_to,
    )
    term_ref[...] = out["term"]
    shift_ref[...] = out["shift"]
    decay_ref[...] = out["decay"]
    base_ref[...] = out["bases"][1]
    last_ref[...] = out["last"]


def ends_of(strip, beyond):
    return jnp.concatenate([strip[16 - beyond : 24], strip[40 : 48 + beyond]], axis=0)


def joined(inner, ends):
    lines, half = inner.shape[0], ends.shape[0] // 2
    return jnp.concatenate([ends[:half], inner[EDGE : lines - EDGE], ends[half:]], axis=0)


def edge_kernel(
    first_ref, starts_ref, sources_ref, params_ref, above_ref, below_ref, weights_ref, rates_ref,
    own_term_ref, own_shift_ref, own_decay_ref,
    terms_ref, factors_ref, shift_ref, decay_ref, base_ref, last_ref, relaxed_ref, halo_ref,
):
    lines = starts_ref.shape[1]
    lane = lax.broadcasted_iota(jnp.int32, (8, LB), 1)
    at = GROUPS * GROUP_ROWS
    own = params_ref[...]
    halo_ref[...] = jnp.zeros_like(halo_ref)
    halo_ref[0, 0:3, :LB] = above_ref[at : at + 3, :LB]
    halo_ref[0, 8:11, :LB] = below_ref[at : at + 3, :LB]
    above, below = halo_ref[0, 0:8, :LB], halo_ref[0, 8:16, :LB]
    upper = jnp.where(lane < SLAB, pltpu.roll(above, SLAB, 1), pltpu.roll(own, SLAB, 1))
    lower = jnp.where(lane < 3 * SLAB, pltpu.roll(own, 3 * SLAB, 1), pltpu.roll(below, 3 * SLAB, 1))
    strip = jnp.where(lane < 2 * SLAB, upper, lower)
    rows = 4 * SLAB
    coupling, *categories = [columns(strip[row : row + 1])[:rows] for row in range(3)]
    coupling = jnp.concatenate([coupling, coupling], axis=1)

    halo_ref[0, 0:16, :] = jnp.zeros((16, 2 * LB), jnp.float32)
    for g in range(GROUPS):
        at = g * GROUP_ROWS
        for index, reach in enumerate(REACH):
            slab = g * len(REACH) + index
            halo_ref[slab, SLAB - reach : SLAB, :] = above_ref[at : at + reach, :]
            halo_ref[slab, SLAB : SLAB + reach, :] = below_ref[at : at + reach, :]
            at += reach

    def strips(slab, low, high):
        return jnp.concatenate([halo_ref[slab, :SLAB, :], low, high, halo_ref[slab, SLAB:, :]], axis=0)

    starts = [
        strips(g * len(REACH), starts_ref[g, :SLAB, :], starts_ref[g, lines - SLAB :, :]) for g in range(GROUPS)
    ]

    def sources(g, m):
        return strips(
            g * len(REACH) + 1 + m, sources_ref[g, m, :SLAB, :], sources_ref[g, m, lines - SLAB :, :]
        )

    def relaxed_to(g, m, field):
        relaxed_ref[g, m] = ends_of(field, 0)

    out = relaxations(starts, sources, coupling, categories, weights_ref[...], rates_ref, first_ref[0, 0], relaxed_to)
    section = lines + 2 * EDGE
    end_decay = ends_of(out["decay"], EDGE)
    decay = joined(own_decay_ref[...], end_decay)
    term = joined(own_term_ref[...], ends_of(out["term"], EDGE))
    for block in range(2):
        at = block * section
        lanes = slice(block * LB, (block + 1) * LB)
        terms_ref[at : at + section, :] = term[:, lanes]
        factors_ref[at : at + section, :] = (decay * decay)[:, lanes]
    shift_ref[...] = joined(own_shift_ref[...], ends_of(out["shift"], EDGE))
    decay_ref[...] = end_decay
    for g in range(GROUPS):
        base_ref[g] = ends_of(out["bases"][g], EDGE)
    last_ref[...] = ends_of(out["last"], 0)


def scan_kernel(place_ref, terms_ref, factors_ref, entering_ref):
    factor = factors_ref[place_ref[0, 0]]
    carried = jnp.zeros_like(factor)
    for d in range(terms_ref.shape[0]):
        entering_ref[d] = carried
        carried = factor * carried + terms_ref[d]


def lines_kernel(params_ref, above_ref, below_ref, coupling_ref, masks_ref, upper_ref):
    lines = params_ref.shape[1]
    at = GROUPS * GROUP_ROWS

    def along(row):
        own = columns(params_ref[row : row + 1, :])
        above = columns(above_ref[at + row : at + row + 1, :LB])
        below = columns(below_ref[at + row : at + row + 1, :LB])
        return jnp.concatenate([above[lines - EDGE :], own, below[:EDGE]], axis=0)

    coupling_ref[...] = along(0)
    even, odd, upper = class_masks([along(1), along(2)])
    for block in range(2):
        masks_ref[0, block] = even[block]
        masks_ref[1, block] = odd[block]
        upper_ref[block] = jnp.where(upper[block], 1.0, 0.0)


def final_kernel(
    first_ref, entering_ref, shift_ref, coupling_ref, masks_ref, upper_ref, weights_ref, starts_ref,
    decay_ref, base_ref, last_ref, relaxed_ref, edge_decay_ref, edge_base_ref, edge_last_ref, edge_relaxed_ref, states_hbm, states_ref, sems,
):
    lines = last_ref.shape[0]
    section = lines + 2 * EDGE
    coupling = jnp.concatenate([coupling_ref[...], coupling_ref[...]], axis=1)
    masks = (
        [masks_ref[0, block] for block in range(2)],
        [masks_ref[1, block] for block in range(2)],
        [upper_ref[block] > 0.5 for block in range(2)],
    )

    entering = jnp.concatenate([entering_ref[:section, :], entering_ref[section:, :]], axis=1)
    shift = shift_ref[...]
    inner = slice(EDGE, EDGE + lines)
    decay = joined(decay_ref[...], edge_decay_ref[...])
    start = jnp.where(first_ref[0, 0] > 0, 0.0, 1.0) * starts_ref[0]
    base = [joined(start, edge_base_ref[0]), joined(base_ref[...], edge_base_ref[1])]
    last = [base[1][inner] + starts_ref[1], joined(last_ref[...], edge_last_ref[...])]
    passed = decay * entering

    def send(g, m):
        copy = pltpu.make_async_copy(states_ref.at[g, m], states_hbm.at[g, m], sems.at[g, m])
        copy.start()
        return copy

    states_ref[0, 3] = passed[inner] + last[0]
    states_ref[1, 3] = (decay * passed)[inner] + last[1]
    copies = [send(g, 3) for g in range(GROUPS)]
    state = [entering + shift - base[0], passed + base[1]]
    weights = weights_ref[...]
    for m in range(STEPS - 1):
        state = solve_lines([spread(s, coupling) for s in state], masks, weights)
        for g in range(GROUPS):
            states_ref[g, m] = joined(relaxed_ref[g, m], edge_relaxed_ref[g, m]) + state[g][inner]
            copies.append(send(g, m))
    for copy in copies:
        copy.wait()


def shards(sources, starts, coupling, classes, inverses, coarse_rate):
    count, along = lax.axis_size("tm"), lax.axis_size("space")
    lines, line_len = starts.shape[1:]
    near_rows = lines + 2 * EDGE
    sections = 2 * near_rows
    f32 = jnp.float32
    place = lax.axis_index("tm").astype(jnp.int32).reshape(1, 1)
    first = (lax.axis_index("tm") == 0).astype(jnp.int32).reshape(1, 1)

    def grant(size):
        return pltpu.CompilerParams(vmem_limit_bytes=size * MEBI)

    def shape(*dims):
        return jax.ShapeDtypeStruct(dims, f32)

    message = shape(MESSAGE_ROWS, line_len)
    up, down, params, held_starts, held_sources, rates, weights = pl.pallas_call(
        pack_kernel,
        out_shape=(
            message,
            message,
            shape(8, lines),
            *[shape(*x.shape) for x in (starts, sources, coarse_rate)],
            jax.ShapeDtypeStruct((4 * LB, 2 * LB), jnp.bfloat16),
        ),
        in_specs=[HBM] * 6,
        out_specs=[VMEM] * 7,
        scratch_shapes=[
            pltpu.VMEM((1, lines), f32),
            pltpu.VMEM((2, lines), jnp.int32),
            pltpu.VMEM(inverses.shape, f32),
            pltpu.SemaphoreType.DMA((4 + GROUPS * (1 + STEPS),)),
        ],
        compiler_params=grant(6),
        name="pack",
    )(*[
        pltpu.with_memory_space_constraint(x, pltpu.HBM)
        for x in (starts, sources, coupling.reshape(1, lines), classes.T, coarse_rate, inverses)
    ])

    with jax.named_scope("halo"):
        upward = [(i, i + 1) for i in range(along - 1)]
        above = lax.ppermute(up, "space", upward)
        below = lax.ppermute(down, "space", [(j, i) for i, j in upward])

    def relaxed(rows):
        return shape(GROUPS, STEPS - 1, rows, line_len)

    term, shift, *own = pl.pallas_call(
        own_kernel,
        out_shape=(*[shape(lines, line_len)] * 5, relaxed(lines)),
        in_specs=[SMEM] + [VMEM] * 5,
        out_specs=[VMEM] * 6,
        compiler_params=grant(24),
        cost_estimate=pl.CostEstimate(flops=5_000_000_000, bytes_accessed=4_000_000, transcendentals=0),
        name="own",
    )(first, held_starts, held_sources, params, weights, rates)
    terms, factors, shift, *edges = pl.pallas_call(
        edge_kernel,
        out_shape=(
            shape(sections, LB),
            shape(sections, LB),
            shape(near_rows, line_len),
            shape(4 * EDGE, line_len),
            shape(GROUPS, 4 * EDGE, line_len),
            shape(2 * EDGE, line_len),
            relaxed(2 * EDGE),
        ),
        in_specs=[SMEM] + [VMEM] * 10,
        out_specs=[VMEM] * 7,
        scratch_shapes=[pltpu.VMEM((GROUPS * len(REACH), 2 * SLAB, line_len), f32)],
        compiler_params=grant(20),
        name="edge",
    )(first, held_starts, held_sources, params, above, below, weights, rates, term, shift, own[0])

    split = (count, 1, sections * LB // count)
    with jax.named_scope("onward"):
        shift = lax.ppermute(shift, "tm", [(i, i + 1) for i in range(count - 1)])
    with jax.named_scope("gather_terms"):
        terms = lax.all_to_all(terms.reshape(split), "tm", 0, 0)
    entering = pl.pallas_call(
        scan_kernel,
        out_shape=shape(*split),
        in_specs=[SMEM] + [VMEM] * 2,
        out_specs=VMEM,
        compiler_params=grant(4),
        name="scan",
    )(place, terms, factors.reshape(split))
    with jax.named_scope("return_terms"):
        entering = lax.all_to_all(entering, "tm", 0, 0)
    spread_lines = pl.pallas_call(
        lines_kernel,
        out_shape=(
            shape(near_rows, LB),
            jax.ShapeDtypeStruct((2, 2, near_rows, LB), jnp.bfloat16),
            shape(2, near_rows, LB),
        ),
        in_specs=[VMEM] * 3,
        out_specs=[VMEM] * 3,
        compiler_params=grant(4),
        cost_estimate=pl.CostEstimate(flops=1_000_000_000, bytes_accessed=1_000_000, transcendentals=0),
        name="lines",
    )(params, above, below)
    return pl.pallas_call(
        final_kernel,
        out_shape=shape(GROUPS, STEPS, lines, line_len),
        in_specs=[SMEM] + [VMEM] * 15,
        out_specs=HBM,
        scratch_shapes=[
            pltpu.VMEM((GROUPS, STEPS, lines, line_len), f32),
            pltpu.SemaphoreType.DMA((GROUPS, STEPS)),
        ],
        compiler_params=grant(20),
        name="final",
    )(first, entering.reshape(sections, LB), shift, *spread_lines, weights, held_starts, *own, *edges)


def solution(mesh):
    in_specs = (
        P("tm", None, "space", None),
        P("tm", "space", None),
        P("space"),
        P("space", None),
        P(),
        P(),
    )
    out_specs = P("tm", None, "space", None)
    return jax.shard_map(shards, mesh=mesh, in_specs=in_specs, out_specs=out_specs, check_vma=False)
```

```python
import functools

import jax
import jax.numpy as jnp
from jax import lax
from jax.experimental import pallas as pl
from jax.experimental.pallas import tpu as pltpu
from jax.sharding import PartitionSpec as P

LB = 128
GROUPS = 2
STEPS = 4
SLAB = 16
EDGE = 8
REACH = (11, 10, 9, 8, 7)
GROUP_ROWS = sum(REACH)
MESSAGE_ROWS = 96
VMEM = pl.BlockSpec(memory_space=pltpu.VMEM)
SMEM = pl.BlockSpec(memory_space=pltpu.SMEM)
HBM = pl.BlockSpec(memory_space=pltpu.HBM)
MEBI = 1024 * 1024


def columns(row):
    return jnp.broadcast_to(row, (LB, LB)).T


def unless(flag_ref):
    return jnp.where(flag_ref[0, 0] > 0, 0.0, 1.0)


def class_masks(categories):
    even, odd, upper = [], [], []
    for category in categories:
        high = category > 1.5
        low = category - jnp.where(high, 2.0, 0.0)
        odd.append(jnp.where(low > 0.5, 1.0, 0.0).astype(jnp.bfloat16))
        even.append(jnp.where(low > 0.5, 0.0, 1.0).astype(jnp.bfloat16))
        upper.append(high)
    return even, odd, upper


def rates_of(categories, rates_ref):
    blocks = []
    for category in categories:
        rate = jnp.broadcast_to(rates_ref[0:1, :], category.shape)
        for c in range(1, 4):
            rate = jnp.where(category > c - 0.5, jnp.broadcast_to(rates_ref[c : c + 1, :], category.shape), rate)
        blocks.append(rate)
    return jnp.concatenate(blocks, axis=1)


def solve_field(field, masks, weights):
    even, odd, upper = masks
    rows = field.shape[0]
    highs, lows = [], []
    for block in range(2):
        x = field[:, block * LB : (block + 1) * LB]
        high = x.astype(jnp.bfloat16)
        low = (x - high.astype(jnp.float32)).astype(jnp.bfloat16)
        highs.append(jnp.concatenate([high * even[block], high * odd[block]], axis=1))
        lows.append(jnp.concatenate([low * even[block], low * odd[block]], axis=1))
    highs, lows = jnp.concatenate(highs, axis=0), jnp.concatenate(lows, axis=0)
    pairs = ((highs, weights[: 2 * LB]), (lows, weights[: 2 * LB]), (highs, weights[2 * LB :]))
    products = [jnp.dot(left, right, preferred_element_type=jnp.float32) for left, right in pairs]
    blocks = []
    for block in range(2):
        parts = [product[block * rows : (block + 1) * rows] for product in products]
        first, second, third = [jnp.where(upper[block], part[:, LB:], part[:, :LB]) for part in parts]
        blocks.append(first + second + third)
    return jnp.concatenate(blocks, axis=1)


def solve_lines(fields, masks, weights):
    return [solve_field(field, masks, weights) for field in fields]


def spread(field, coupling):
    rows = field.shape[0]
    return field + coupling * (pltpu.roll(field, 1, 0) + pltpu.roll(field, rows - 1, 0))


def relaxations(starts, sources, coupling, categories, weights, rates_ref, first, relaxed_to):
    masks = class_masks(categories)
    linear, state = starts[0], starts
    for m in range(STEPS):
        *state, linear = solve_lines(
            [spread(state[g], coupling) + sources(g, m) for g in range(GROUPS)] + [spread(linear, coupling)],
            masks,
            weights,
        )
        if m < STEPS - 1:
            for g in range(GROUPS):
                relaxed_to(g, m, state[g])
    ends = state
    linear = jnp.where(first > 0, jnp.zeros_like(linear), linear)
    change = ends[0] - starts[1]
    resid, onward = change, ends[1]
    for m in range(STEPS):
        resid, onward = solve_lines([spread(resid, coupling), spread(onward, coupling)], masks, weights)
    rates = rates_of(categories, rates_ref)
    decay = jnp.exp(-rates)
    ahead = onward * jnp.exp(rates)
    held = decay * linear
    return dict(
        term=resid + ahead - held,
        shift=ends[1] - ahead,
        decay=decay,
        bases=(jnp.where(first > 0, jnp.zeros_like(linear), starts[0]), change - linear),
        last=ends[1] + resid - held,
    )


def pack_kernel(
    starts_hbm, sources_hbm, coupling_hbm, classes_hbm, rates_hbm, inverses_hbm,
    up_ref, down_ref, params_ref, starts_ref, sources_ref, rates_ref, weights_ref,
    coupling_row, classes_rows, inverses_ref, sems,
):
    lines = starts_hbm.shape[1]
    pairs = [
        (inverses_hbm, inverses_ref),
        (coupling_hbm, coupling_row),
        (classes_hbm, classes_rows),
        *[(starts_hbm.at[g], starts_ref.at[g]) for g in range(GROUPS)],
        *[(sources_hbm.at[g, m], sources_ref.at[g, m]) for g in range(GROUPS) for m in range(STEPS)],
        (rates_hbm, rates_ref),
    ]
    copies = [pltpu.make_async_copy(src, dst, sems.at[i]) for i, (src, dst) in enumerate(pairs)]
    for copy in copies:
        copy.start()
    for ref in (up_ref, down_ref, params_ref):
        ref[...] = jnp.zeros_like(ref)
    for copy in copies[:3]:
        copy.wait()
    params_ref[0:1, :] = coupling_row[...]
    params_ref[1:3, :] = classes_rows[...].astype(jnp.float32)
    for c in range(4):
        transposed = inverses_ref[c].T
        rounded = transposed.astype(jnp.bfloat16)
        rest = (transposed - rounded.astype(jnp.float32)).astype(jnp.bfloat16)
        row, lane = c % 2 * LB, c // 2 * LB
        weights_ref[row : row + LB, lane : lane + LB] = rounded
        weights_ref[2 * LB + row : 3 * LB + row, lane : lane + LB] = rest
    for copy in copies[3:]:
        copy.wait()
    for g in range(GROUPS):
        at = g * GROUP_ROWS
        for index, reach in enumerate(REACH):
            if index == 0:
                own = starts_ref.at[g]
            else:
                own = sources_ref.at[g, index - 1]
            up_ref[at : at + reach, :] = own[lines - reach :, :]
            down_ref[at : at + reach, :] = own[:reach, :]
            at += reach
    for ref in (up_ref, down_ref):
        ref[GROUPS * GROUP_ROWS : GROUPS * GROUP_ROWS + 3, :LB] = params_ref[0:3, :]


def own_kernel(
    first_ref, starts_ref, sources_ref, params_ref, weights_ref, rates_ref,
    term_ref, shift_ref, decay_ref, base_ref, last_ref, relaxed_ref,
):
    coupling, *categories = [columns(params_ref[row : row + 1, :]) for row in range(3)]
    coupling = jnp.concatenate([coupling, coupling], axis=1)

    def relaxed_to(g, m, field):
        relaxed_ref[g, m] = field

    out = relaxations(
        [starts_ref[g] for g in range(GROUPS)], lambda g, m: sources_ref[g, m], coupling, categories, weights_ref[...],
        rates_ref, first_ref[0, 0], relaxed_to,
    )
    term_ref[...] = out["term"]
    shift_ref[...] = out["shift"]
    decay_ref[...] = out["decay"]
    base_ref[...] = out["bases"][1]
    last_ref[...] = out["last"]


def ends_of(strip, beyond):
    return jnp.concatenate([strip[16 - beyond : 24], strip[40 : 48 + beyond]], axis=0)


def joined(inner, ends):
    lines, half = inner.shape[0], ends.shape[0] // 2
    return jnp.concatenate([ends[:half], inner[EDGE : lines - EDGE], ends[half:]], axis=0)


def edge_kernel(
    first_ref, top_ref, bottom_ref, starts_ref, sources_ref, params_ref, above_ref, below_ref, weights_ref, rates_ref,
    own_term_ref, own_shift_ref, own_decay_ref,
    terms_ref, factors_ref, shift_ref, decay_ref, base_ref, last_ref, relaxed_ref, halo_ref,
):
    lines = starts_ref.shape[1]
    lane = lax.broadcasted_iota(jnp.int32, (8, LB), 1)
    at = GROUPS * GROUP_ROWS
    own = params_ref[...]
    keep_above, keep_below = unless(top_ref), unless(bottom_ref)
    halo_ref[...] = jnp.zeros_like(halo_ref)
    halo_ref[0, 0:3, :LB] = keep_above * above_ref[at : at + 3, :LB]
    halo_ref[0, 8:11, :LB] = keep_below * below_ref[at : at + 3, :LB]
    above, below = halo_ref[0, 0:8, :LB], halo_ref[0, 8:16, :LB]
    upper = jnp.where(lane < SLAB, pltpu.roll(above, SLAB, 1), pltpu.roll(own, SLAB, 1))
    lower = jnp.where(lane < 3 * SLAB, pltpu.roll(own, 3 * SLAB, 1), pltpu.roll(below, 3 * SLAB, 1))
    strip = jnp.where(lane < 2 * SLAB, upper, lower)
    rows = 4 * SLAB
    coupling, *categories = [columns(strip[row : row + 1])[:rows] for row in range(3)]
    coupling = jnp.concatenate([coupling, coupling], axis=1)

    halo_ref[0, 0:16, :] = jnp.zeros((16, 2 * LB), jnp.float32)
    for g in range(GROUPS):
        at = g * GROUP_ROWS
        for index, reach in enumerate(REACH):
            slab = g * len(REACH) + index
            halo_ref[slab, SLAB - reach : SLAB, :] = keep_above * above_ref[at : at + reach, :]
            halo_ref[slab, SLAB : SLAB + reach, :] = keep_below * below_ref[at : at + reach, :]
            at += reach

    def strips(slab, low, high):
        return jnp.concatenate([halo_ref[slab, :SLAB, :], low, high, halo_ref[slab, SLAB:, :]], axis=0)

    starts = [
        strips(g * len(REACH), starts_ref[g, :SLAB, :], starts_ref[g, lines - SLAB :, :]) for g in range(GROUPS)
    ]

    def sources(g, m):
        return strips(
            g * len(REACH) + 1 + m, sources_ref[g, m, :SLAB, :], sources_ref[g, m, lines - SLAB :, :]
        )

    def relaxed_to(g, m, field):
        relaxed_ref[g, m] = ends_of(field, 0)

    out = relaxations(starts, sources, coupling, categories, weights_ref[...], rates_ref, first_ref[0, 0], relaxed_to)
    section = lines + 2 * EDGE
    end_decay = ends_of(out["decay"], EDGE)
    decay = joined(own_decay_ref[...], end_decay)
    term = joined(own_term_ref[...], ends_of(out["term"], EDGE))
    for block in range(2):
        at = block * section
        lanes = slice(block * LB, (block + 1) * LB)
        terms_ref[at : at + section, :] = term[:, lanes]
        factors_ref[at : at + section, :] = (decay * decay)[:, lanes]
    shift_ref[...] = joined(own_shift_ref[...], ends_of(out["shift"], EDGE))
    decay_ref[...] = end_decay
    for g in range(GROUPS):
        base_ref[g] = ends_of(out["bases"][g], EDGE)
    last_ref[...] = ends_of(out["last"], 0)


def scan_kernel(place_ref, terms_ref, factors_ref, entering_ref):
    factor = factors_ref[place_ref[0, 0]]
    carried = jnp.zeros_like(factor)
    for d in range(terms_ref.shape[0]):
        entering_ref[d] = carried
        carried = factor * carried + terms_ref[d]


def lines_kernel(top_ref, bottom_ref, params_ref, above_ref, below_ref, coupling_ref, masks_ref, upper_ref):
    lines = params_ref.shape[1]
    at = GROUPS * GROUP_ROWS

    def along(row):
        own = columns(params_ref[row : row + 1, :])
        above = columns(unless(top_ref) * above_ref[at + row : at + row + 1, :LB])
        below = columns(unless(bottom_ref) * below_ref[at + row : at + row + 1, :LB])
        return jnp.concatenate([above[lines - EDGE :], own, below[:EDGE]], axis=0)

    coupling_ref[...] = along(0)
    even, odd, upper = class_masks([along(1), along(2)])
    for block in range(2):
        masks_ref[0, block] = even[block]
        masks_ref[1, block] = odd[block]
        upper_ref[block] = jnp.where(upper[block], 1.0, 0.0)


def final_kernel(
    first_ref, entering_ref, shift_ref, coupling_ref, masks_ref, upper_ref, weights_ref, starts_ref,
    decay_ref, base_ref, last_ref, relaxed_ref, edge_decay_ref, edge_base_ref, edge_last_ref, edge_relaxed_ref, states_hbm, states_ref, sems,
):
    lines = last_ref.shape[0]
    section = lines + 2 * EDGE
    coupling = jnp.concatenate([coupling_ref[...], coupling_ref[...]], axis=1)
    masks = (
        [masks_ref[0, block] for block in range(2)],
        [masks_ref[1, block] for block in range(2)],
        [upper_ref[block] > 0.5 for block in range(2)],
    )

    entering = jnp.concatenate([entering_ref[:section, :], entering_ref[section:, :]], axis=1)
    keep = unless(first_ref)
    shift = keep * shift_ref[...]
    inner = slice(EDGE, EDGE + lines)
    decay = joined(decay_ref[...], edge_decay_ref[...])
    start = keep * starts_ref[0]
    base = [joined(start, edge_base_ref[0]), joined(base_ref[...], edge_base_ref[1])]
    last = [base[1][inner] + starts_ref[1], joined(last_ref[...], edge_last_ref[...])]
    passed = decay * entering

    def send(g, m):
        copy = pltpu.make_async_copy(states_ref.at[g, m], states_hbm.at[g, m], sems.at[g, m])
        copy.start()
        return copy

    states_ref[0, 3] = passed[inner] + last[0]
    states_ref[1, 3] = (decay * passed)[inner] + last[1]
    copies = [send(g, 3) for g in range(GROUPS)]
    state = [entering + shift - base[0], passed + base[1]]
    weights = weights_ref[...]
    for m in range(STEPS - 1):
        state = solve_lines([spread(s, coupling) for s in state], masks, weights)
        for g in range(GROUPS):
            states_ref[g, m] = joined(relaxed_ref[g, m], edge_relaxed_ref[g, m]) + state[g][inner]
            copies.append(send(g, m))
    for copy in copies:
        copy.wait()


def shards(sources, starts, coupling, classes, inverses, coarse_rate):
    count, along = lax.axis_size("tm"), lax.axis_size("space")
    lines, line_len = starts.shape[1:]
    near_rows = lines + 2 * EDGE
    sections = 2 * near_rows
    f32 = jnp.float32
    place = lax.axis_index("tm").astype(jnp.int32).reshape(1, 1)
    row = lax.axis_index("space")
    first, top, bottom = [
        flag.astype(jnp.int32).reshape(1, 1) for flag in (lax.axis_index("tm") == 0, row == 0, row == along - 1)
    ]

    def grant(size):
        return pltpu.CompilerParams(vmem_limit_bytes=size * MEBI)

    def shape(*dims):
        return jax.ShapeDtypeStruct(dims, f32)

    message = shape(MESSAGE_ROWS, line_len)
    up, down, params, held_starts, held_sources, rates, weights = pl.pallas_call(
        pack_kernel,
        out_shape=(
            message,
            message,
            shape(8, lines),
            *[shape(*x.shape) for x in (starts, sources, coarse_rate)],
            jax.ShapeDtypeStruct((4 * LB, 2 * LB), jnp.bfloat16),
        ),
        in_specs=[HBM] * 6,
        out_specs=[VMEM] * 7,
        scratch_shapes=[
            pltpu.VMEM((1, lines), f32),
            pltpu.VMEM((2, lines), jnp.int32),
            pltpu.VMEM(inverses.shape, f32),
            pltpu.SemaphoreType.DMA((4 + GROUPS * (1 + STEPS),)),
        ],
        compiler_params=grant(6),
        name="pack",
    )(*[
        pltpu.with_memory_space_constraint(x, pltpu.HBM)
        for x in (starts, sources, coupling.reshape(1, lines), classes.T, coarse_rate, inverses)
    ])

    with jax.named_scope("halo"):
        upward = [(i, (i + 1) % along) for i in range(along)]
        above = lax.ppermute(up, "space", upward)
        below = lax.ppermute(down, "space", [(j, i) for i, j in upward])

    def relaxed(rows):
        return shape(GROUPS, STEPS - 1, rows, line_len)

    term, shift, *own = pl.pallas_call(
        own_kernel,
        out_shape=(*[shape(lines, line_len)] * 5, relaxed(lines)),
        in_specs=[SMEM] + [VMEM] * 5,
        out_specs=[VMEM] * 6,
        compiler_params=grant(24),
        cost_estimate=pl.CostEstimate(flops=5_000_000_000, bytes_accessed=4_000_000, transcendentals=0),
        name="own",
    )(first, held_starts, held_sources, params, weights, rates)
    terms, factors, shift, *edges = pl.pallas_call(
        edge_kernel,
        out_shape=(
            shape(sections, LB),
            shape(sections, LB),
            shape(near_rows, line_len),
            shape(4 * EDGE, line_len),
            shape(GROUPS, 4 * EDGE, line_len),
            shape(2 * EDGE, line_len),
            relaxed(2 * EDGE),
        ),
        in_specs=[SMEM] * 3 + [VMEM] * 10,
        out_specs=[VMEM] * 7,
        scratch_shapes=[pltpu.VMEM((GROUPS * len(REACH), 2 * SLAB, line_len), f32)],
        compiler_params=grant(20),
        name="edge",
    )(first, top, bottom, held_starts, held_sources, params, above, below, weights, rates, term, shift, own[0])

    split = (count, 1, sections * LB // count)
    with jax.named_scope("onward"):
        shift = lax.ppermute(shift, "tm", [(i, (i + 1) % count) for i in range(count)])
    with jax.named_scope("gather_terms"):
        terms = lax.all_to_all(terms.reshape(split), "tm", 0, 0)
    entering = pl.pallas_call(
        scan_kernel,
        out_shape=shape(*split),
        in_specs=[SMEM] + [VMEM] * 2,
        out_specs=VMEM,
        compiler_params=grant(4),
        name="scan",
    )(place, terms, factors.reshape(split))
    with jax.named_scope("return_terms"):
        entering = lax.all_to_all(entering, "tm", 0, 0)
    spread_lines = pl.pallas_call(
        lines_kernel,
        out_shape=(
            shape(near_rows, LB),
            jax.ShapeDtypeStruct((2, 2, near_rows, LB), jnp.bfloat16),
            shape(2, near_rows, LB),
        ),
        in_specs=[SMEM] * 2 + [VMEM] * 3,
        out_specs=[VMEM] * 3,
        compiler_params=grant(4),
        cost_estimate=pl.CostEstimate(flops=1_000_000_000, bytes_accessed=1_000_000, transcendentals=0),
        name="lines",
    )(top, bottom, params, above, below)
    return pl.pallas_call(
        final_kernel,
        out_shape=shape(GROUPS, STEPS, lines, line_len),
        in_specs=[SMEM] + [VMEM] * 15,
        out_specs=HBM,
        scratch_shapes=[
            pltpu.VMEM((GROUPS, STEPS, lines, line_len), f32),
            pltpu.SemaphoreType.DMA((GROUPS, STEPS)),
        ],
        compiler_params=grant(20),
        name="final",
    )(first, entering.reshape(sections, LB), shift, *spread_lines, weights, held_starts, *own, *edges)


def solution(mesh):
    in_specs = (
        P("tm", None, "space", None),
        P("tm", "space", None),
        P("space"),
        P("space", None),
        P(),
        P(),
    )
    out_specs = P("tm", None, "space", None)
    return jax.shard_map(shards, mesh=mesh, in_specs=in_specs, out_specs=out_specs, check_vma=False)
```

```python
import functools

import jax
import jax.numpy as jnp
from jax import lax
from jax.experimental import pallas as pl
from jax.experimental.pallas import tpu as pltpu
from jax.sharding import PartitionSpec as P

LB = 128
GROUPS = 2
STEPS = 4
SLAB = 16
EDGE = 8
REACH = (11, 10, 9, 8, 7)
GROUP_ROWS = sum(REACH)
MESSAGE_ROWS = 96
VMEM = pl.BlockSpec(memory_space=pltpu.VMEM)
SMEM = pl.BlockSpec(memory_space=pltpu.SMEM)
HBM = pl.BlockSpec(memory_space=pltpu.HBM)
MEBI = 1024 * 1024


def columns(row):
    return jnp.broadcast_to(row, (LB, LB)).T


def unless(flag_ref):
    return jnp.where(flag_ref[0, 0] > 0, 0.0, 1.0)


def class_masks(categories):
    even, odd, upper = [], [], []
    for category in categories:
        high = category > 1.5
        low = category - jnp.where(high, 2.0, 0.0)
        odd.append(jnp.where(low > 0.5, 1.0, 0.0).astype(jnp.bfloat16))
        even.append(jnp.where(low > 0.5, 0.0, 1.0).astype(jnp.bfloat16))
        upper.append(high)
    return even, odd, upper


def rates_of(categories, rates_ref):
    blocks = []
    for category in categories:
        rate = jnp.broadcast_to(rates_ref[0:1, :], category.shape)
        for c in range(1, 4):
            rate = jnp.where(category > c - 0.5, jnp.broadcast_to(rates_ref[c : c + 1, :], category.shape), rate)
        blocks.append(rate)
    return jnp.concatenate(blocks, axis=1)


def solve_field(field, masks, weights):
    even, odd, upper = masks
    rows = field.shape[0]
    highs, lows = [], []
    for block in range(2):
        x = field[:, block * LB : (block + 1) * LB]
        high = x.astype(jnp.bfloat16)
        low = (x - high.astype(jnp.float32)).astype(jnp.bfloat16)
        highs.append(jnp.concatenate([high * even[block], high * odd[block]], axis=1))
        lows.append(jnp.concatenate([low * even[block], low * odd[block]], axis=1))
    highs, lows = jnp.concatenate(highs, axis=0), jnp.concatenate(lows, axis=0)
    pairs = ((highs, weights[: 2 * LB]), (lows, weights[: 2 * LB]), (highs, weights[2 * LB :]))
    products = [jnp.dot(left, right, preferred_element_type=jnp.float32) for left, right in pairs]
    blocks = []
    for block in range(2):
        parts = [product[block * rows : (block + 1) * rows] for product in products]
        first, second, third = [jnp.where(upper[block], part[:, LB:], part[:, :LB]) for part in parts]
        blocks.append(first + second + third)
    return jnp.concatenate(blocks, axis=1)


def solve_lines(fields, masks, weights):
    return [solve_field(field, masks, weights) for field in fields]


def spread(field, coupling):
    rows = field.shape[0]
    return field + coupling * (pltpu.roll(field, 1, 0) + pltpu.roll(field, rows - 1, 0))


def relaxations(starts, sources, coupling, categories, weights, rates_ref, first, relaxed_to):
    masks = class_masks(categories)
    linear, state = starts[0], starts
    for m in range(STEPS):
        *state, linear = solve_lines(
            [spread(state[g], coupling) + sources(g, m) for g in range(GROUPS)] + [spread(linear, coupling)],
            masks,
            weights,
        )
        if m < STEPS - 1:
            for g in range(GROUPS):
                relaxed_to(g, m, state[g])
    ends = state
    linear = jnp.where(first > 0, jnp.zeros_like(linear), linear)
    change = ends[0] - starts[1]
    resid, onward = change, ends[1]
    for m in range(STEPS):
        resid, onward = solve_lines([spread(resid, coupling), spread(onward, coupling)], masks, weights)
    rates = rates_of(categories, rates_ref)
    decay = jnp.exp(-rates)
    ahead = onward * jnp.exp(rates)
    held = decay * linear
    return dict(
        term=resid + ahead - held,
        shift=ends[1] - ahead,
        bases=(jnp.where(first > 0, jnp.zeros_like(linear), starts[0]), change - linear),
        last=ends[1] + resid - held,
    )


def pack_kernel(
    starts_hbm, sources_hbm, coupling_hbm, classes_hbm, rates_hbm, inverses_hbm,
    up_ref, down_ref, params_ref, starts_ref, sources_ref, rates_ref, weights_ref,
    coupling_row, classes_rows, inverses_ref, sems,
):
    lines = starts_hbm.shape[1]
    pairs = [
        (inverses_hbm, inverses_ref),
        (coupling_hbm, coupling_row),
        (classes_hbm, classes_rows),
        *[(starts_hbm.at[g], starts_ref.at[g]) for g in range(GROUPS)],
        *[(sources_hbm.at[g, m], sources_ref.at[g, m]) for g in range(GROUPS) for m in range(STEPS)],
        (rates_hbm, rates_ref),
    ]
    copies = [pltpu.make_async_copy(src, dst, sems.at[i]) for i, (src, dst) in enumerate(pairs)]
    for copy in copies:
        copy.start()
    for ref in (up_ref, down_ref, params_ref):
        ref[...] = jnp.zeros_like(ref)
    for copy in copies[:3]:
        copy.wait()
    params_ref[0:1, :] = coupling_row[...]
    params_ref[1:3, :] = classes_rows[...].astype(jnp.float32)
    for c in range(4):
        transposed = inverses_ref[c].T
        rounded = transposed.astype(jnp.bfloat16)
        rest = (transposed - rounded.astype(jnp.float32)).astype(jnp.bfloat16)
        row, lane = c % 2 * LB, c // 2 * LB
        weights_ref[row : row + LB, lane : lane + LB] = rounded
        weights_ref[2 * LB + row : 3 * LB + row, lane : lane + LB] = rest
    for copy in copies[3:]:
        copy.wait()
    for g in range(GROUPS):
        at = g * GROUP_ROWS
        for index, reach in enumerate(REACH):
            if index == 0:
                own = starts_ref.at[g]
            else:
                own = sources_ref.at[g, index - 1]
            up_ref[at : at + reach, :] = own[lines - reach :, :]
            down_ref[at : at + reach, :] = own[:reach, :]
            at += reach
    for ref in (up_ref, down_ref):
        ref[GROUPS * GROUP_ROWS : GROUPS * GROUP_ROWS + 3, :LB] = params_ref[0:3, :]


def own_kernel(
    first_ref, starts_ref, sources_ref, params_ref, weights_ref, rates_ref,
    term_ref, shift_ref, base_ref, last_ref, relaxed_ref,
):
    coupling, *categories = [columns(params_ref[row : row + 1, :]) for row in range(3)]
    coupling = jnp.concatenate([coupling, coupling], axis=1)

    def relaxed_to(g, m, field):
        relaxed_ref[g, m] = field

    out = relaxations(
        [starts_ref[g] for g in range(GROUPS)], lambda g, m: sources_ref[g, m], coupling, categories, weights_ref[...],
        rates_ref, first_ref[0, 0], relaxed_to,
    )
    term_ref[...] = out["term"]
    shift_ref[...] = out["shift"]
    base_ref[...] = out["bases"][1]
    last_ref[...] = out["last"]


def ends_of(strip, beyond):
    return jnp.concatenate([strip[16 - beyond : 24], strip[40 : 48 + beyond]], axis=0)


def joined(inner, ends):
    lines, half = inner.shape[0], ends.shape[0] // 2
    return jnp.concatenate([ends[:half], inner[EDGE : lines - EDGE], ends[half:]], axis=0)


def edge_kernel(
    first_ref, top_ref, bottom_ref, starts_ref, sources_ref, params_ref, above_ref, below_ref, weights_ref, rates_ref,
    own_term_ref, own_shift_ref,
    terms_ref, shift_ref, base_ref, last_ref, relaxed_ref, halo_ref,
):
    lines = starts_ref.shape[1]
    lane = lax.broadcasted_iota(jnp.int32, (8, LB), 1)
    at = GROUPS * GROUP_ROWS
    own = params_ref[...]
    keep_above, keep_below = unless(top_ref), unless(bottom_ref)
    halo_ref[...] = jnp.zeros_like(halo_ref)
    halo_ref[0, 0:3, :LB] = keep_above * above_ref[at : at + 3, :LB]
    halo_ref[0, 8:11, :LB] = keep_below * below_ref[at : at + 3, :LB]
    above, below = halo_ref[0, 0:8, :LB], halo_ref[0, 8:16, :LB]
    upper = jnp.where(lane < SLAB, pltpu.roll(above, SLAB, 1), pltpu.roll(own, SLAB, 1))
    lower = jnp.where(lane < 3 * SLAB, pltpu.roll(own, 3 * SLAB, 1), pltpu.roll(below, 3 * SLAB, 1))
    strip = jnp.where(lane < 2 * SLAB, upper, lower)
    rows = 4 * SLAB
    coupling, *categories = [columns(strip[row : row + 1])[:rows] for row in range(3)]
    coupling = jnp.concatenate([coupling, coupling], axis=1)

    halo_ref[0, 0:16, :] = jnp.zeros((16, 2 * LB), jnp.float32)
    for g in range(GROUPS):
        at = g * GROUP_ROWS
        for index, reach in enumerate(REACH):
            slab = g * len(REACH) + index
            halo_ref[slab, SLAB - reach : SLAB, :] = keep_above * above_ref[at : at + reach, :]
            halo_ref[slab, SLAB : SLAB + reach, :] = keep_below * below_ref[at : at + reach, :]
            at += reach

    def strips(slab, low, high):
        return jnp.concatenate([halo_ref[slab, :SLAB, :], low, high, halo_ref[slab, SLAB:, :]], axis=0)

    starts = [
        strips(g * len(REACH), starts_ref[g, :SLAB, :], starts_ref[g, lines - SLAB :, :]) for g in range(GROUPS)
    ]

    def sources(g, m):
        return strips(
            g * len(REACH) + 1 + m, sources_ref[g, m, :SLAB, :], sources_ref[g, m, lines - SLAB :, :]
        )

    def relaxed_to(g, m, field):
        relaxed_ref[g, m] = ends_of(field, 0)

    out = relaxations(starts, sources, coupling, categories, weights_ref[...], rates_ref, first_ref[0, 0], relaxed_to)
    section = lines + 2 * EDGE
    term = joined(own_term_ref[...], ends_of(out["term"], EDGE))
    for block in range(2):
        at = block * section
        lanes = slice(block * LB, (block + 1) * LB)
        terms_ref[at : at + section, :] = term[:, lanes]
    shift_ref[...] = joined(own_shift_ref[...], ends_of(out["shift"], EDGE))
    for g in range(GROUPS):
        base_ref[g] = ends_of(out["bases"][g], EDGE)
    last_ref[...] = ends_of(out["last"], 0)


def scan_kernel(place_ref, terms_ref, factors_ref, shift_ref, entering_ref):
    del shift_ref
    factor = factors_ref[place_ref[0, 0]]
    carried = jnp.zeros_like(factor)
    for d in range(terms_ref.shape[0]):
        entering_ref[d] = carried
        carried = factor * carried + terms_ref[d]


def lines_kernel(
    top_ref, bottom_ref, params_ref, above_ref, below_ref, rates_ref,
    coupling_ref, masks_ref, upper_ref, decay_ref, factors_ref,
):
    lines = params_ref.shape[1]
    at = GROUPS * GROUP_ROWS

    def along(row):
        own = columns(params_ref[row : row + 1, :])
        above = columns(unless(top_ref) * above_ref[at + row : at + row + 1, :LB])
        below = columns(unless(bottom_ref) * below_ref[at + row : at + row + 1, :LB])
        return jnp.concatenate([above[lines - EDGE :], own, below[:EDGE]], axis=0)

    coupling_ref[...] = along(0)
    categories = [along(1), along(2)]
    even, odd, upper = class_masks(categories)
    decay = jnp.exp(-rates_of(categories, rates_ref))
    decay_ref[...] = decay
    for block in range(2):
        section = lines + 2 * EDGE
        lanes = slice(block * LB, (block + 1) * LB)
        factors_ref[block * section : (block + 1) * section, :] = (decay * decay)[:, lanes]
        masks_ref[0, block] = even[block]
        masks_ref[1, block] = odd[block]
        upper_ref[block] = jnp.where(upper[block], 1.0, 0.0)


def final_kernel(
    first_ref, entering_ref, shift_ref, coupling_ref, masks_ref, upper_ref, decay_ref, weights_ref, starts_ref,
    base_ref, last_ref, relaxed_ref, edge_base_ref, edge_last_ref, edge_relaxed_ref, states_hbm, states_ref, sems,
):
    lines = last_ref.shape[0]
    section = lines + 2 * EDGE
    coupling = jnp.concatenate([coupling_ref[...], coupling_ref[...]], axis=1)
    masks = (
        [masks_ref[0, block] for block in range(2)],
        [masks_ref[1, block] for block in range(2)],
        [upper_ref[block] > 0.5 for block in range(2)],
    )

    entering = jnp.concatenate([entering_ref[:section, :], entering_ref[section:, :]], axis=1)
    keep = unless(first_ref)
    shift = keep * shift_ref[...]
    inner = slice(EDGE, EDGE + lines)
    decay = decay_ref[...]
    start = keep * starts_ref[0]
    base = [joined(start, edge_base_ref[0]), joined(base_ref[...], edge_base_ref[1])]
    last = [base[1][inner] + starts_ref[1], joined(last_ref[...], edge_last_ref[...])]
    passed = decay * entering

    def send(g, m):
        copy = pltpu.make_async_copy(states_ref.at[g, m], states_hbm.at[g, m], sems.at[g, m])
        copy.start()
        return copy

    states_ref[0, 3] = passed[inner] + last[0]
    states_ref[1, 3] = (decay * passed)[inner] + last[1]
    copies = [send(g, 3) for g in range(GROUPS)]
    state = [entering + shift - base[0], passed + base[1]]
    weights = weights_ref[...]
    for m in range(STEPS - 1):
        state = solve_lines([spread(s, coupling) for s in state], masks, weights)
        for g in range(GROUPS):
            states_ref[g, m] = joined(relaxed_ref[g, m], edge_relaxed_ref[g, m]) + state[g][inner]
            copies.append(send(g, m))
    for copy in copies:
        copy.wait()


def shards(sources, starts, coupling, classes, inverses, coarse_rate):
    count, along = lax.axis_size("tm"), lax.axis_size("space")
    lines, line_len = starts.shape[1:]
    near_rows = lines + 2 * EDGE
    sections = 2 * near_rows
    f32 = jnp.float32
    place = lax.axis_index("tm").astype(jnp.int32).reshape(1, 1)
    row = lax.axis_index("space")
    first, top, bottom = [
        flag.astype(jnp.int32).reshape(1, 1) for flag in (lax.axis_index("tm") == 0, row == 0, row == along - 1)
    ]

    def grant(size):
        return pltpu.CompilerParams(vmem_limit_bytes=size * MEBI)

    def shape(*dims):
        return jax.ShapeDtypeStruct(dims, f32)

    message = shape(MESSAGE_ROWS, line_len)
    up, down, params, held_starts, held_sources, rates, weights = pl.pallas_call(
        pack_kernel,
        out_shape=(
            message,
            message,
            shape(8, lines),
            *[shape(*x.shape) for x in (starts, sources, coarse_rate)],
            jax.ShapeDtypeStruct((4 * LB, 2 * LB), jnp.bfloat16),
        ),
        in_specs=[HBM] * 6,
        out_specs=[VMEM] * 7,
        scratch_shapes=[
            pltpu.VMEM((1, lines), f32),
            pltpu.VMEM((2, lines), jnp.int32),
            pltpu.VMEM(inverses.shape, f32),
            pltpu.SemaphoreType.DMA((4 + GROUPS * (1 + STEPS),)),
        ],
        compiler_params=grant(6),
        name="pack",
    )(*[
        pltpu.with_memory_space_constraint(x, pltpu.HBM)
        for x in (starts, sources, coupling.reshape(1, lines), classes.T, coarse_rate, inverses)
    ])

    with jax.named_scope("halo"):
        upward = [(i, (i + 1) % along) for i in range(along)]
        above = lax.ppermute(up, "space", upward)
        below = lax.ppermute(down, "space", [(j, i) for i, j in upward])

    def relaxed(rows):
        return shape(GROUPS, STEPS - 1, rows, line_len)

    term, shift, *own = pl.pallas_call(
        own_kernel,
        out_shape=(*[shape(lines, line_len)] * 4, relaxed(lines)),
        in_specs=[SMEM] + [VMEM] * 5,
        out_specs=[VMEM] * 5,
        compiler_params=grant(24),
        cost_estimate=pl.CostEstimate(flops=5_000_000_000, bytes_accessed=4_000_000, transcendentals=0),
        name="own",
    )(first, held_starts, held_sources, params, weights, rates)
    terms, shift, *edges = pl.pallas_call(
        edge_kernel,
        out_shape=(
            shape(sections, LB),
            shape(near_rows, line_len),
            shape(GROUPS, 4 * EDGE, line_len),
            shape(2 * EDGE, line_len),
            relaxed(2 * EDGE),
        ),
        in_specs=[SMEM] * 3 + [VMEM] * 9,
        out_specs=[VMEM] * 5,
        scratch_shapes=[pltpu.VMEM((GROUPS * len(REACH), 2 * SLAB, line_len), f32)],
        compiler_params=grant(20),
        name="edge",
    )(first, top, bottom, held_starts, held_sources, params, above, below, weights, rates, term, shift)

    split = (count, 1, sections * LB // count)
    with jax.named_scope("onward"):
        shift = lax.ppermute(shift, "tm", [(i, (i + 1) % count) for i in range(count)])
    with jax.named_scope("gather_terms"):
        terms = lax.all_to_all(terms.reshape(split), "tm", 0, 0)
    *spread_lines, factors = pl.pallas_call(
        lines_kernel,
        out_shape=(
            shape(near_rows, LB),
            jax.ShapeDtypeStruct((2, 2, near_rows, LB), jnp.bfloat16),
            shape(2, near_rows, LB),
            shape(near_rows, line_len),
            shape(sections, LB),
        ),
        in_specs=[SMEM] * 2 + [VMEM] * 4,
        out_specs=[VMEM] * 5,
        compiler_params=grant(4),
        cost_estimate=pl.CostEstimate(flops=1_000_000_000, bytes_accessed=1_000_000, transcendentals=0),
        name="lines",
    )(top, bottom, params, above, below, rates)
    entering = pl.pallas_call(
        scan_kernel,
        out_shape=shape(*split),
        in_specs=[SMEM] + [VMEM] * 3,
        out_specs=VMEM,
        compiler_params=grant(4),
        name="scan",
    )(place, terms, factors.reshape(split), shift)
    with jax.named_scope("return_terms"):
        entering = lax.all_to_all(entering, "tm", 0, 0)
    return pl.pallas_call(
        final_kernel,
        out_shape=shape(GROUPS, STEPS, lines, line_len),
        in_specs=[SMEM] + [VMEM] * 14,
        out_specs=HBM,
        scratch_shapes=[
            pltpu.VMEM((GROUPS, STEPS, lines, line_len), f32),
            pltpu.SemaphoreType.DMA((GROUPS, STEPS)),
        ],
        compiler_params=grant(20),
        name="final",
    )(first, entering.reshape(sections, LB), shift, *spread_lines, weights, held_starts, *own, *edges)


def solution(mesh):
    in_specs = (
        P("tm", None, "space", None),
        P("tm", "space", None),
        P("space"),
        P("space", None),
        P(),
        P(),
    )
    out_specs = P("tm", None, "space", None)
    return jax.shard_map(shards, mesh=mesh, in_specs=in_specs, out_specs=out_specs, check_vma=False)
```
